128 devices in a mesh: elem: 4 (over z), reg: 32 (over x, y, core).
Axes of the slice: x: 4, y: 4, z: 4, core: 2. Of those that a mesh axis runs over, the one named last changes fastest.
Arguments:
- rf: bfloat16 [32, 1024, 2048], P('reg', 'elem'), may hold values from -12 to 12
- tx_delay: int32 [32, 128, 512], replicated, may hold values from 1 to 1022
- rx_delay: int32 [128, 1024], P(None, 'elem'), may hold values from 0 to 1021, as said below
- aperture: int32 [128, 4], replicated, may hold values from 0 to 32, as said below
Outputs:
- image: float32 [128, 512], P('reg', 'elem')
The draws below stay inside these ranges and needn't reach their ends.
Inputs may be any that keep to these rules, and one draw needn't show every extreme that they name: `aperture`: rows and columns are half-open ranges of the probe, each spanning 8 or more elements; some region has the whole probe. `rx_delay`: each receive delay is a delay of the region plus a delay of the element alone.
All inputs are finite; a program needn't handle non-finite values.
Results may differ from the reference program's by a relative error of at most 0.007.
Values may be sent and summed in bfloat16 or wider, within the bound.
No kernel may reach another device: no remote copies, remote signals or barrier semaphores. Data moves between devices by JAX's collectives and lax.ppermute only.
A program may use at most 448 MiB of HBM per device.

```python
import math
import jax
import jax.numpy as jnp
from jax import lax

PROBE = 32
SUB = 8
VOXR = 512
SAMPLES = 2048
ELEMS = 1024
TX = 32
REGIONS = 128
N_ELEM = 4


def lens_delay():
    element = jnp.arange(ELEMS, dtype=jnp.int32)
    row = element // PROBE
    column = element % PROBE
    return (((2 * row - PROBE + 1) ** 2 + (2 * column - PROBE + 1) ** 2) // (2 * PROBE)).astype(jnp.int32)


def draw_aperture(key, part):
    key = jax.random.fold_in(key, 11)
    keys = jax.random.split(key, 5)
    row_mid = jax.random.randint(keys[0], (REGIONS,), 0, PROBE)
    col_mid = jax.random.randint(keys[1], (REGIONS,), 0, PROBE)
    row_half = jax.random.randint(keys[2], (REGIONS,), SUB // 2, PROBE // 2 + 1)
    col_half = jax.random.randint(keys[3], (REGIONS,), SUB // 2, PROBE // 2 + 1)
    row_lo = jnp.clip(row_mid - row_half, 0, PROBE - SUB)
    row_hi = jnp.maximum(row_lo + SUB, jnp.minimum(row_mid + row_half, PROBE))
    col_lo = jnp.clip(col_mid - col_half, 0, PROBE - SUB)
    col_hi = jnp.maximum(col_lo + SUB, jnp.minimum(col_mid + col_half, PROBE))
    chosen = jax.random.randint(keys[4], (), 0, REGIONS)
    whole = jnp.arange(REGIONS) == chosen
    row_lo = jnp.where(whole, 0, row_lo)
    col_lo = jnp.where(whole, 0, col_lo)
    row_hi = jnp.where(whole, PROBE, row_hi)
    col_hi = jnp.where(whole, PROBE, col_hi)
    return jnp.stack([row_lo, row_hi, col_lo, col_hi], axis=-1).astype(jnp.int32)


def draw_rx_delay(key, part):
    key = jax.random.fold_in(key, 23)
    keys = jax.random.split(key, 2)
    offset = jax.random.randint(keys[0], (REGIONS,), 0, SAMPLES // 2 - PROBE)
    chosen = jax.random.randint(keys[1], (), 0, REGIONS)
    index = jnp.arange(REGIONS, dtype=jnp.int32)
    offset = jnp.where(index == chosen, SAMPLES // 2 - PROBE - 1, offset)
    offset = jnp.where(index == (chosen + 1) % REGIONS, 0, offset)
    return (offset[:, None] + lens_delay()[None, :]).astype(jnp.int32)


def draw_rf(key, part):
    key = jax.random.fold_in(key, 37)
    keys = jax.random.split(key, 8)
    extent = SAMPLES + PROBE
    noise = jnp.clip(jax.random.normal(keys[0], (TX, PROBE, PROBE, extent), jnp.float32), -5.0, 5.0)
    gain = jnp.exp(jax.random.uniform(keys[1], (PROBE, PROBE), jnp.float32, -0.22, 0.22))
    across = jax.random.uniform(keys[2], (PROBE, PROBE), jnp.float32, 0.3, 0.8)
    downward = jax.random.uniform(keys[3], (PROBE, PROBE), jnp.float32, 0.3, 0.8)
    field = noise + across[None, :, :, None] * jnp.roll(noise, -1, axis=2) + downward[None, :, :, None] * jnp.roll(noise, -1, axis=1)
    field = (gain[None, :, :, None] * field).reshape(TX, ELEMS, extent)
    lens = lens_delay()
    starts = (PROBE - lens).astype(jnp.int32)
    aligned = jax.vmap(lambda trace, begin: lax.dynamic_slice_in_dim(trace, begin, SAMPLES, 1), in_axes=(1, 0), out_axes=1)(field, starts)
    element = jnp.arange(ELEMS, dtype=jnp.int32)
    row = (element // PROBE).astype(jnp.float32)
    column = (element % PROBE).astype(jnp.float32)
    sample = jnp.arange(SAMPLES, dtype=jnp.float32)
    omega = jax.random.uniform(keys[4], (2,), jnp.float32, 0.4, 1.2)
    steer = jax.random.uniform(keys[5], (2, 2), jnp.float32, 0.5, 1.3) * jnp.array([[1.0, -1.0], [-1.0, 1.0]], jnp.float32)
    amps = jax.random.uniform(keys[6], (2, TX), jnp.float32, 0.6, 1.2)
    phase = jax.random.uniform(keys[7], (2, TX), jnp.float32, -jnp.pi, jnp.pi)
    total = aligned
    for which in range(2):
        element_phase = steer[which, 0] * column + steer[which, 1] * row - omega[which] * lens.astype(jnp.float32)
        angle = omega[which] * sample[None, None, :] + element_phase[None, :, None] + phase[which][:, None, None]
        total = total + amps[which][:, None, None] * jnp.cos(angle)
    return jnp.clip(total, -12.0, 12.0).astype(jnp.bfloat16)


def plant(values, key, smallest, high):
    shape = values.shape
    spot = [jax.random.randint(jax.random.fold_in(key, axis), (), 0, shape[axis]) for axis in range(len(shape))]
    values = values.at[tuple(spot)].set(smallest)
    longest = shape.index(max(shape))
    spot[longest] = (spot[longest] + 1) % shape[longest]
    return values.at[tuple(spot)].set(high)


def setup_inputs(seed: int = 0) -> dict:
    streams_of = jax.random.split(jax.random.key(seed), 5)
    return {
        "rf": draw_rf(jax.random.fold_in(streams_of[4], 71), 0),
        "tx_delay": plant(jax.random.randint(streams_of[1], (TX, REGIONS, VOXR), 1, SAMPLES // 2 - 1), jax.random.fold_in(streams_of[1], 1), 1, (SAMPLES // 2 - 1) - 1).astype(jnp.int32),
        "rx_delay": draw_rx_delay(jax.random.fold_in(streams_of[4], 71), 0),
        "aperture": draw_aperture(jax.random.fold_in(streams_of[4], 71), 0),
    }


tap_weights = (-0.0625, 0.5625, 0.5625, -0.0625)
load_factor = 0.05

def aperture_mask(bounds, first, width):
    element = first + jnp.arange(width, dtype=jnp.int32)
    row = (element // PROBE)[None, :]
    column = (element % PROBE)[None, :]
    inside = (row >= bounds[:, 0:1]) & (row < bounds[:, 1:2])
    return inside & (column >= bounds[:, 2:3]) & (column < bounds[:, 3:4])

def delay_tiles(signals, tx_part, rx_part, inside):
    count, width, samples = signals.shape
    flat = signals.reshape(count, width * samples)
    offsets = (jnp.arange(width, dtype=jnp.int32) * samples)[None, None, None, :]
    where_at = tx_part[:, :, :, None] + rx_part[None, :, None, :] + offsets
    total = jnp.zeros(where_at.shape, jnp.float32)
    for place, weight in enumerate(tap_weights):
        picked = jax.vmap(lambda table, spots: table[spots])(flat, where_at + (place - 1))
        total = total + weight * picked.astype(jnp.float32)
    return jnp.where(inside[None, :, None, :], total, 0.0).astype(jnp.bfloat16)

def window_table():
    column = jnp.arange(PROBE, dtype=jnp.int32)[:, None]
    start = jnp.arange(SUB, dtype=jnp.int32)[None, :]
    return ((column >= start) & (column <= start + PROBE - SUB)).astype(jnp.float32)

def band_stats(tiles):
    wide = tiles.astype(jnp.float32)
    count, regions, voxels, width = wide.shape
    gram = jnp.einsum('tkvi,tkvj->kij', wide, wide, precision=lax.Precision.HIGHEST)
    smooth = jnp.einsum('tkvac,cp->kvap', wide.reshape(count, regions, voxels, width // PROBE, PROBE), window_table(), precision=lax.Precision.HIGHEST)
    return (gram, smooth)

def fold_cov(gram):
    regions = gram.shape[0]
    split = gram.reshape(regions, SUB, PROBE, SUB, PROBE)
    total = split[:, :, 0:SUB, :, 0:SUB]
    for shift in range(1, PROBE - SUB + 1):
        total = total + split[:, :, shift:shift + SUB, :, shift:shift + SUB]
    return total.reshape(regions, SUB * SUB, SUB * SUB)

def mvdr_weights(cov):
    regions, order, _ = cov.shape
    trace = jnp.trace(cov, axis1=1, axis2=2)
    loaded = cov + (load_factor * trace / order)[:, None, None] * jnp.eye(order, dtype=jnp.float32)[None]
    factor = jnp.linalg.cholesky(loaded)
    ones = jnp.ones((regions, order, 1), jnp.float32)
    middle = lax.linalg.triangular_solve(factor, ones, left_side=True, lower=True)
    solved = lax.linalg.triangular_solve(factor, middle, left_side=True, lower=True, transpose_a=True)[..., 0]
    return solved / lax.optimization_barrier(jnp.sum(solved, axis=-1, keepdims=True))

def reference(rf, tx_delay, rx_delay, aperture):
    width = SUB * PROBE
    scale = 8.0 / math.sqrt(TX * N_ELEM * (PROBE - SUB + 1))

    def one_region(region):
        tx_part = lax.dynamic_slice_in_dim(tx_delay, region, 1, 1)
        rx_part = lax.dynamic_slice_in_dim(rx_delay, region, 1, 0)
        bounds = lax.dynamic_slice_in_dim(aperture, region, 1, 0)
        cov = jnp.zeros((1, SUB * SUB, SUB * SUB), jnp.float32)
        smooth = jnp.zeros((1, VOXR, SUB, SUB), jnp.float32)
        for band in range(N_ELEM):
            lower = band * width
            tiles = delay_tiles(rf[:, lower:lower + width], tx_part, rx_part[:, lower:lower + width], aperture_mask(bounds, lower, width))
            gram, part = band_stats(tiles)
            cov = cov + fold_cov(gram)
            smooth = smooth + part
        weights = mvdr_weights(cov)
        return (lax.optimization_barrier(jnp.sum(smooth.reshape(1, VOXR, SUB * SUB) * weights[:, None, :], axis=-1)) * scale)[0]
    return lax.map(one_region, jnp.arange(REGIONS, dtype=jnp.int32))
```

```python
import functools
import math

import jax
import jax.numpy as jnp
from jax import lax
from jax.experimental import pallas as pl
from jax.experimental.pallas import tpu as pltpu
from jax.sharding import PartitionSpec as P

PROBE = 32
SUB = 8
SHIFTS = PROBE - SUB + 1
WIDTH = SUB * PROBE
ORDER = SUB * SUB
LANES = 128

tap_weights = (-0.0625, 0.5625, 0.5625, -0.0625)
load_factor = 0.05

DELTAS = (0, 1, 2, 3, 4, -4, -5, -6, -7)
TILES = 17


def lane_iota(shape):
    return lax.broadcasted_iota(jnp.int32, shape, len(shape) - 1)


def row_iota(shape):
    return lax.broadcasted_iota(jnp.int32, shape, 0)


def window_matrix(delta, half):
    element = row_iota((WIDTH, LANES))
    lane = lane_iota((WIDTH, LANES))
    target = lane - ORDER * half
    x = target & (SUB - 1)
    k = element & (PROBE - 1)
    good = (target >= 0) & (target < ORDER)
    good &= (element // PROBE) == (target // SUB)
    good &= (k >= x) & (k <= x + PROBE - SUB)
    good &= (x + delta >= 0) & (x + delta < SUB)
    return good.astype(jnp.float32).astype(jnp.bfloat16)


def split(x):
    high = x.astype(jnp.bfloat16)
    low = (x - high.astype(jnp.float32)).astype(jnp.bfloat16)
    return high, low


def stats_kernel(place, rf_ref, tx_ref, rx_ref, aperture_ref, cov_ref, traces_ref,
                 wide, shifted, count32, count16, colmask, windows):
    regions = rx_ref.shape[0]
    samples = rf_ref.shape[-1]
    blocks = samples // LANES
    voxels = tx_ref.shape[-1]
    first_row = place[1] * SUB

    rx = rx_ref[...].astype(jnp.float32)
    base = jnp.min(rx, axis=1, keepdims=True)
    lead = rx[0:1, :] - base[0:1, :]
    relative = jnp.transpose(jnp.broadcast_to(lead, (LANES, WIDTH))).astype(jnp.int32)
    wide[0:SUB, :] = jnp.zeros((SUB, samples), jnp.float32)
    wide[SUB + WIDTH : 2 * SUB + WIDTH, :] = jnp.zeros((SUB, samples), jnp.float32)
    step = 32
    for chunk in range(WIDTH // step):
        rows = slice(chunk * step, (chunk + 1) * step)
        x = rf_ref[0, rows, :].astype(jnp.float32)
        y = tap_weights[0] * pltpu.roll(x, 1, 1)
        y = y + tap_weights[1] * x
        y = y + tap_weights[2] * pltpu.roll(x, samples - 1, 1)
        y = y + tap_weights[3] * pltpu.roll(x, samples - 2, 1)
        y = y.astype(jnp.bfloat16).astype(jnp.float32)
        move = relative[rows, :]
        fine = move & (LANES - 1)
        reach = lane_iota((step, LANES)) + fine
        spot = reach & (LANES - 1)
        parts = [
            jnp.take_along_axis(y[:, j * LANES : (j + 1) * LANES], spot, axis=1)
            for j in range(blocks)
        ]
        stay = reach < LANES
        parts = [jnp.where(stay, parts[j], parts[(j + 1) % blocks]) for j in range(blocks)]
        for bit in range(3):
            here = (move & (LANES << bit)) != 0
            parts = [
                jnp.where(here, parts[(j + (1 << bit)) % blocks], parts[j]) for j in range(blocks)
            ]
        for j in range(blocks):
            wide[SUB + chunk * step : SUB + (chunk + 1) * step, j * LANES : (j + 1) * LANES] = parts[j]
    for which, delta in enumerate(DELTAS):
        for chunk in range(WIDTH // step):
            begin = SUB + chunk * step + delta
            part = wide[begin : begin + step, :].astype(jnp.bfloat16)
            shifted[which, chunk * step : (chunk + 1) * step, :] = part
            shifted[which, WIDTH + chunk * step : WIDTH + (chunk + 1) * step, :] = part
            if which == 0:
                traces_ref[chunk * step : (chunk + 1) * step, :] = part

    sums = tx_ref[0] + base.astype(jnp.int32)
    tall = 16
    high_rows = row_iota((tall, voxels))
    low_rows = row_iota((LANES, voxels))
    for r in range(regions):
        spots = sums[r : r + 1, :]
        high = jnp.where(spots // LANES == high_rows, 1.0, 0.0).astype(jnp.bfloat16)
        low = jnp.where((spots & (LANES - 1)) == low_rows, 1.0, 0.0).astype(jnp.bfloat16)
        count32[:, r, :] = lax.dot_general(
            high, low, (((1,), (1,)), ((), ())), preferred_element_type=jnp.float32
        )
    for j in range(blocks):
        count16[:, j * LANES : (j + 1) * LANES] = count32[j].astype(jnp.bfloat16)

    lane = lane_iota((regions, WIDTH))
    row = lane // PROBE
    column = lane & (PROBE - 1)
    bounds = aperture_ref[...]
    row_lo, row_hi = bounds[:, 0:1] - first_row, bounds[:, 1:2] - first_row
    col_lo, col_hi = bounds[:, 2:3], bounds[:, 3:4]
    for which, delta in enumerate(DELTAS):
        other = column + delta
        inside = (column >= col_lo) & (column < col_hi) & (other >= col_lo) & (other < col_hi)
        colmask[which] = inside.astype(jnp.float32)
    row_inside = (row >= row_lo) & (row < row_hi)

    def row_mask(da):
        other = (row + da) & (SUB - 1)
        return (row_inside & (other >= row_lo) & (other < row_hi)).astype(jnp.float32)

    for slot, (delta, half) in enumerate(
        ((1, 0), (-7, 0), (2, 1), (-6, 1), (3, 0), (-5, 0), (3, 1), (-5, 1), (4, 0), (-4, 0), (0, 1))
    ):
        windows[slot] = window_matrix(delta, half)

    def term(delta, da, rows, slot):
        which = DELTAS.index(delta)
        begin = pl.multiple_of(da * PROBE, PROBE)
        pair = shifted[0, 0:WIDTH, :] * shifted[which, pl.ds(begin, WIDTH), :]
        gram = lax.dot_general(
            count16[...], pair, (((1,), (1,)), ((), ())), preferred_element_type=jnp.float32
        )
        gram = gram * (colmask[which] * rows)
        high, low = split(gram)
        out = jnp.dot(high, windows[slot], preferred_element_type=jnp.float32)
        return out + jnp.dot(low, windows[slot], preferred_element_type=jnp.float32)

    def put(tile, value):
        cov_ref[:, pl.ds(pl.multiple_of(tile * LANES, LANES), LANES)] = value

    @pl.loop(0, SUB)
    def _(da):
        rows = row_mask(da)
        put(da, term(1, da, rows, 0) + term(-7, da, rows, 1) + term(2, da, rows, 2) + term(-6, da, rows, 3))

    @pl.loop(0, SUB // 2)
    def _(da):
        rows = row_mask(da)
        more = row_mask(da + 4)
        put(
            SUB + da,
            term(3, da, rows, 4) + term(-5, da, rows, 5) + term(3, da + 4, more, 6) + term(-5, da + 4, more, 7),
        )

    @pl.loop(0, SUB // 2 + 1)
    def _(da):
        rows = row_mask(da)
        put(12 + da, term(4, da, rows, 8) + term(-4, da, rows, 9) + term(0, da, rows, 10))


def stats(place, rf, tx_delay, rx_delay, aperture):
    regions = rx_delay.shape[0]
    samples = rf.shape[-1]
    voxels = tx_delay.shape[-1]
    grid_spec = pltpu.PrefetchScalarGridSpec(
        num_scalar_prefetch=1,
        grid=(1,),
        in_specs=[
            pl.BlockSpec(rf.shape, lambda i, place: (0, 0, 0)),
            pl.BlockSpec((1, regions, voxels), lambda i, place: (place[0], 0, 0)),
            pl.BlockSpec(rx_delay.shape, lambda i, place: (0, 0)),
            pl.BlockSpec(aperture.shape, lambda i, place: (0, 0)),
        ],
        out_specs=[
            pl.BlockSpec((regions, TILES * LANES), lambda i, place: (0, 0)),
            pl.BlockSpec((WIDTH, samples), lambda i, place: (0, 0)),
        ],
        scratch_shapes=[
            pltpu.VMEM((WIDTH + 2 * SUB, samples), jnp.float32),
            pltpu.VMEM((len(DELTAS), 2 * WIDTH, samples), jnp.bfloat16),
            pltpu.VMEM((16, regions, LANES), jnp.float32),
            pltpu.VMEM((regions, samples), jnp.bfloat16),
            pltpu.VMEM((len(DELTAS), regions, WIDTH), jnp.float32),
            pltpu.VMEM((11, WIDTH, LANES), jnp.bfloat16),
        ],
    )
    return pl.pallas_call(
        stats_kernel,
        grid_spec=grid_spec,
        out_shape=[
            jax.ShapeDtypeStruct((regions, TILES * LANES), jnp.float32),
            jax.ShapeDtypeStruct((WIDTH, samples), jnp.bfloat16),
        ],
        compiler_params=pltpu.CompilerParams(vmem_limit_bytes=56 * 1024 * 1024),
        name="stats",
    )(place, rf, tx_delay, rx_delay, aperture)


def solve_kernel(parts_ref, weights_ref):
    total = jnp.sum(parts_ref[...], axis=0, keepdims=True)
    tiles = [total[:, t * LANES : (t + 1) * LANES] for t in range(TILES)]
    tall = jnp.concatenate(tiles + [jnp.zeros((LANES - TILES, LANES), jnp.float32)], axis=0)
    turned = jnp.transpose(tall)
    table = jnp.concatenate([turned[0:ORDER, 0:ORDER], turned[ORDER:LANES, 0:ORDER]], axis=1)
    i = row_iota((ORDER, LANES))
    lane = lane_iota((ORDER, LANES))
    j = lane & (ORDER - 1)
    da = ((j // SUB) - (i // SUB)) & (SUB - 1)
    d = ((j & (SUB - 1)) - (i & (SUB - 1))) & (SUB - 1)
    spot = jnp.where(
        d == 1, da,
        jnp.where(
            d == 2, da + ORDER,
            jnp.where(
                d == 3, SUB + (da & 3) + ORDER * (da // 4),
                jnp.where(d == 4, 12 + da, 12 + da + ORDER),
            ),
        ),
    )
    stored = ((d >= 1) & (d <= 3)) | (((d == 0) | (d == 4)) & (da <= 4))
    half = jnp.take_along_axis(table, spot & (LANES - 1), axis=1)
    half = jnp.where(stored & (lane < ORDER), half, 0.0)
    square = jnp.concatenate([half, jnp.zeros((LANES - ORDER, LANES), jnp.float32)], axis=0)
    cov = jnp.where(stored, half, jnp.transpose(square)[0:ORDER, :])
    diagonal = lane == i
    trace = jnp.sum(jnp.sum(jnp.where(diagonal, cov, 0.0), axis=1, keepdims=True), axis=0, keepdims=True)
    cov = cov + jnp.where(diagonal, load_factor * trace / ORDER, 0.0)
    work = jnp.where(lane < ORDER, cov, 1.0)
    column = i[:, 0:1]
    for k in range(ORDER):
        pivot_row = work[k : k + 1, :]
        inverse = 1.0 / pivot_row[:, k : k + 1]
        factor = jnp.where(column == k, 0.0, work[:, k : k + 1] * inverse)
        work = work - factor * pivot_row
    held = jnp.sum(jnp.where(diagonal, work, 0.0), axis=1, keepdims=True)
    solved = work[:, ORDER : ORDER + 1] / held
    row = jnp.sum(jnp.where(diagonal, solved, 0.0), axis=0, keepdims=True)
    weights_ref[...] = row / jnp.sum(row, axis=1, keepdims=True)


def solve(parts):
    return pl.pallas_call(
        solve_kernel,
        out_shape=jax.ShapeDtypeStruct((1, LANES), jnp.float32),
        compiler_params=pltpu.CompilerParams(vmem_limit_bytes=32 * 1024 * 1024),
        name="solve",
    )(parts)


def image_kernel(place, weights_ref, traces_ref, tx_ref, rx_ref, aperture_ref, out_ref, line_ref):
    regions = rx_ref.shape[0]
    samples = traces_ref.shape[-1]
    voxels = tx_ref.shape[-1]
    first_row = place[1] * SUB

    source = row_iota((LANES, WIDTH))
    element = lane_iota((LANES, WIDTH))
    x = source & (SUB - 1)
    k = element & (PROBE - 1)
    spread = (source // SUB == element // PROBE) & (k >= x) & (k <= x + PROBE - SUB)
    spread = spread.astype(jnp.float32).astype(jnp.bfloat16)
    weights = weights_ref[...]
    high, low = split(weights)
    rest = (weights - high.astype(jnp.float32) - low.astype(jnp.float32)).astype(jnp.bfloat16)
    gain = jnp.dot(high, spread, preferred_element_type=jnp.float32)
    gain = gain + jnp.dot(low, spread, preferred_element_type=jnp.float32)
    gain = gain + jnp.dot(rest, spread, preferred_element_type=jnp.float32)
    lane = lane_iota((regions, WIDTH))
    row = lane // PROBE + first_row
    column = lane & (PROBE - 1)
    bounds = aperture_ref[...]
    inside = (row >= bounds[:, 0:1]) & (row < bounds[:, 1:2])
    inside &= (column >= bounds[:, 2:3]) & (column < bounds[:, 3:4])
    high, low = split(jnp.where(inside, gain, 0.0))
    line_ref[...] = jnp.dot(high, traces_ref[...], preferred_element_type=jnp.float32) + jnp.dot(
        low, traces_ref[...], preferred_element_type=jnp.float32
    )

    base = jnp.min(rx_ref[...].astype(jnp.float32), axis=1, keepdims=True).astype(jnp.int32)
    sums = tx_ref[0] + base
    group = 32
    for begin in range(0, regions, group):
        rows = slice(begin, begin + group)
        for v in range(voxels // LANES):
            spots = sums[rows, v * LANES : (v + 1) * LANES]
            fine = spots & (LANES - 1)
            coarse = spots // LANES
            picked = jnp.zeros((group, LANES), jnp.float32)
            for j in range(samples // LANES):
                found = jnp.take_along_axis(line_ref[rows, j * LANES : (j + 1) * LANES], fine, axis=1)
                picked = jnp.where(coarse == j, found, picked)
            out_ref[rows, v * LANES : (v + 1) * LANES] = picked


def image(place, weights, traces, tx_delay, rx_delay, aperture):
    regions = rx_delay.shape[0]
    samples = traces.shape[-1]
    voxels = tx_delay.shape[-1]
    grid_spec = pltpu.PrefetchScalarGridSpec(
        num_scalar_prefetch=1,
        grid=(1,),
        in_specs=[
            pl.BlockSpec(weights.shape, lambda i, place: (0, 0)),
            pl.BlockSpec(traces.shape, lambda i, place: (0, 0)),
            pl.BlockSpec((1, regions, voxels), lambda i, place: (place[0], 0, 0)),
            pl.BlockSpec(rx_delay.shape, lambda i, place: (0, 0)),
            pl.BlockSpec(aperture.shape, lambda i, place: (0, 0)),
        ],
        out_specs=pl.BlockSpec((regions, voxels), lambda i, place: (0, 0)),
        scratch_shapes=[pltpu.VMEM((regions, samples), jnp.float32)],
    )
    return pl.pallas_call(
        image_kernel,
        grid_spec=grid_spec,
        out_shape=jax.ShapeDtypeStruct((regions, voxels), jnp.float32),
        compiler_params=pltpu.CompilerParams(vmem_limit_bytes=32 * 1024 * 1024),
        name="image",
    )(place, weights, traces, tx_delay, rx_delay, aperture)


BOTH = ("reg", "elem")


def per_device(rf, tx_delay, rx_delay, aperture):
    n_reg = lax.axis_size("reg")
    n_elem = lax.axis_size("elem")
    regions, voxels = rx_delay.shape[0], tx_delay.shape[2]
    devices = n_reg * n_elem
    scale = 8.0 / math.sqrt(n_reg * n_elem * SHIFTS)
    place = jnp.stack([lax.axis_index("reg"), lax.axis_index("elem")]).astype(jnp.int32)
    cov, traces = stats(place, rf, tx_delay, rx_delay, aperture)
    parts = lax.all_to_all(cov, BOTH, 0, 0, tiled=True)
    mine = solve(parts)
    weights = lax.all_to_all(jnp.broadcast_to(mine, (devices, LANES)), BOTH, 0, 0, tiled=True)
    partial = image(place, weights, traces, tx_delay, rx_delay, aperture)
    owned = partial.reshape(n_reg, regions // n_reg, n_elem, voxels // n_elem).transpose(0, 2, 1, 3)
    owned = owned.reshape(devices, regions // n_reg, voxels // n_elem)
    arrived = lax.all_to_all(owned, BOTH, 0, 0, tiled=True)
    return jnp.sum(arrived, axis=0) * scale


def solution(mesh):
    in_specs = (P("reg", "elem", None), P(), P(None, "elem"), P())
    out_specs = P("reg", "elem")
    return jax.shard_map(
        per_device, mesh=mesh, in_specs=in_specs, out_specs=out_specs, check_vma=False
    )
```

```python
import functools
import math

import jax
import jax.numpy as jnp
from jax import lax
from jax.experimental import pallas as pl
from jax.experimental.pallas import tpu as pltpu
from jax.sharding import PartitionSpec as P

PROBE = 32
SUB = 8
SHIFTS = PROBE - SUB + 1
WIDTH = SUB * PROBE
ORDER = SUB * SUB
LANES = 128

tap_weights = (-0.0625, 0.5625, 0.5625, -0.0625)
load_factor = 0.05

DELTAS = (0, 1, 2, 3, 4, -4, -5, -6, -7)
TILES = 17
WINDOWS = ((1, 0), (-7, 0), (2, 1), (-6, 1), (3, 0), (-5, 0), (3, 1), (-5, 1), (4, 0), (-4, 0), (0, 1))


def lane_iota(shape):
    return lax.broadcasted_iota(jnp.int32, shape, len(shape) - 1)


def row_iota(shape):
    return lax.broadcasted_iota(jnp.int32, shape, 0)


def window_matrix(delta, half):
    element = lane_iota((LANES, WIDTH))
    target = row_iota((LANES, WIDTH)) - ORDER * half
    x = target & (SUB - 1)
    k = element & (PROBE - 1)
    good = (target >= 0) & (target < ORDER)
    good &= (element // PROBE) == (target // SUB)
    good &= (k >= x) & (k <= x + PROBE - SUB)
    good &= (x + delta >= 0) & (x + delta < SUB)
    return good.astype(jnp.float32).astype(jnp.bfloat16)


def split(x):
    high = x.astype(jnp.bfloat16)
    low = (x - high.astype(jnp.float32)).astype(jnp.bfloat16)
    return high, low


def stats_kernel(elem, reg, rf_ref, tx_ref, rx_ref, aperture_ref, cov_ref, traces_ref, spots_ref,
                 wide, shifted, count32, count16, colmask, rowmask, windows, grams):
    del reg
    regions = rx_ref.shape[0]
    samples = rf_ref.shape[-1]
    blocks = samples // LANES
    voxels = tx_ref.shape[-1]
    first_row = elem[0] * SUB

    rx = rx_ref[...].astype(jnp.float32)
    base = jnp.min(rx, axis=1, keepdims=True)
    lead = rx[0:1, :] - base[0:1, :]
    relative = jnp.transpose(jnp.broadcast_to(lead, (LANES, WIDTH))).astype(jnp.int32)
    wide[0:SUB, :] = jnp.zeros((SUB, samples), jnp.float32)
    wide[SUB + WIDTH : 2 * SUB + WIDTH, :] = jnp.zeros((SUB, samples), jnp.float32)
    step = 32
    for chunk in range(WIDTH // step):
        rows = slice(chunk * step, (chunk + 1) * step)
        x = rf_ref[0, rows, :].astype(jnp.float32)
        y = tap_weights[0] * pltpu.roll(x, 1, 1)
        y = y + tap_weights[1] * x
        y = y + tap_weights[2] * pltpu.roll(x, samples - 1, 1)
        y = y + tap_weights[3] * pltpu.roll(x, samples - 2, 1)
        y = y.astype(jnp.bfloat16).astype(jnp.float32)
        move = relative[rows, :]
        fine = move & (LANES - 1)
        reach = lane_iota((step, LANES)) + fine
        spot = reach & (LANES - 1)
        parts = [
            jnp.take_along_axis(y[:, j * LANES : (j + 1) * LANES], spot, axis=1)
            for j in range(blocks)
        ]
        stay = reach < LANES
        parts = [jnp.where(stay, parts[j], parts[(j + 1) % blocks]) for j in range(blocks)]
        for bit in range(3):
            here = (move & (LANES << bit)) != 0
            parts = [
                jnp.where(here, parts[(j + (1 << bit)) % blocks], parts[j]) for j in range(blocks)
            ]
        for j in range(blocks):
            wide[SUB + chunk * step : SUB + (chunk + 1) * step, j * LANES : (j + 1) * LANES] = parts[j]

    def shift_rows(which, chunk):
        begin = SUB + DELTAS[which]
        if isinstance(chunk, int):
            part = wide[begin + chunk * step : begin + (chunk + 1) * step, :]
        else:
            around = wide[pl.ds(pl.multiple_of(chunk * step, step), step + 2 * SUB), :]
            part = around[begin : begin + step]
        part = part.astype(jnp.bfloat16)
        for copy in range(2):
            shifted[which, pl.ds(pl.multiple_of(copy * WIDTH + chunk * step, step), step), :] = part
        return part

    for chunk in range(WIDTH // step):
        traces_ref[chunk * step : (chunk + 1) * step, :] = shift_rows(0, chunk)
        shift_rows(1, chunk)

    sums = tx_ref[0] + base.astype(jnp.int32)
    spots_ref[...] = sums
    tall = 16
    high_rows = row_iota((tall, voxels))
    low_rows = row_iota((LANES, voxels))
    for r in range(regions):
        spots = sums[r : r + 1, :]
        high = jnp.where(spots // LANES == high_rows, 1.0, 0.0).astype(jnp.bfloat16)
        low = jnp.where((spots & (LANES - 1)) == low_rows, 1.0, 0.0).astype(jnp.bfloat16)
        count32[:, r, :] = lax.dot_general(
            high, low, (((1,), (1,)), ((), ())), preferred_element_type=jnp.float32
        )
    for j in range(blocks):
        count16[j * LANES : (j + 1) * LANES, :] = jnp.transpose(count32[j]).astype(jnp.bfloat16)

    element = row_iota((WIDTH, regions))
    row = element // PROBE
    column = element & (PROBE - 1)
    bounds = aperture_ref[...]
    row_lo, row_hi = bounds[0:1, :] - first_row, bounds[1:2, :] - first_row
    col_lo, col_hi = bounds[2:3, :], bounds[3:4, :]
    column_inside = (column >= col_lo) & (column < col_hi)
    for which, delta in enumerate(DELTAS):
        other = column + delta
        inside = column_inside & (other >= col_lo) & (other < col_hi)
        colmask[which] = inside.astype(jnp.float32).astype(jnp.bfloat16)
    row_inside = (row >= row_lo) & (row < row_hi)
    for da in range(SUB):
        other = (row + da) & (SUB - 1)
        inside = row_inside & (other >= row_lo) & (other < row_hi)
        rowmask[da] = inside.astype(jnp.float32).astype(jnp.bfloat16)

    for slot, (delta, half) in enumerate(WINDOWS):
        windows[slot] = window_matrix(delta, half)

    for which, delta in enumerate(DELTAS):
        reach = SUB if delta in (1, 2, 3, -5, -6, -7) else SUB // 2 + 1
        if 1 <= which < len(DELTAS) - 1:
            for chunk in range(WIDTH // step):
                shift_rows(which + 1, chunk)
        lead_rows = shifted[0, 0:WIDTH, :]
        pairs = [
            lead_rows * shifted[which, da * PROBE : da * PROBE + WIDTH, :] for da in range(reach)
        ]
        gram = jnp.dot(
            jnp.concatenate(pairs, axis=0), count16[...], preferred_element_type=jnp.float32
        ).astype(jnp.bfloat16)
        for da in range(reach):
            grams[which, da] = gram[da * WIDTH : (da + 1) * WIDTH] * colmask[which] * rowmask[da]

    def put(tile, terms):
        left = jnp.concatenate([windows[WINDOWS.index((delta, half))] for delta, half, da in terms], axis=1)
        right = jnp.concatenate([grams[DELTAS.index(delta), da] for delta, half, da in terms], axis=0)
        out = jnp.dot(left, right, preferred_element_type=jnp.float32)
        cov_ref[:, tile * LANES : (tile + 1) * LANES] = jnp.transpose(out).astype(cov_ref.dtype)

    for da in range(SUB):
        put(da, ((1, 0, da), (-7, 0, da), (2, 1, da), (-6, 1, da)))
    for da in range(SUB // 2):
        put(SUB + da, ((3, 0, da), (-5, 0, da), (3, 1, da + 4), (-5, 1, da + 4)))
    for da in range(SUB // 2 + 1):
        put(12 + da, ((4, 0, da), (-4, 0, da), (0, 1, da)))


def stats(elem, reg, rf, tx_delay, rx_delay, aperture):
    regions = rx_delay.shape[0]
    samples = rf.shape[-1]
    voxels = tx_delay.shape[-1]
    grid_spec = pltpu.PrefetchScalarGridSpec(
        num_scalar_prefetch=2,
        grid=(1,),
        in_specs=[
            pl.BlockSpec(rf.shape, lambda i, elem, reg: (0, 0, 0)),
            pl.BlockSpec((1, regions, voxels), lambda i, elem, reg: (reg[0], 0, 0)),
            pl.BlockSpec(rx_delay.shape, lambda i, elem, reg: (0, 0)),
            pl.BlockSpec(aperture.shape, lambda i, elem, reg: (0, 0)),
        ],
        out_specs=[
            pl.BlockSpec((regions, TILES * LANES), lambda i, elem, reg: (0, 0)),
            pl.BlockSpec((WIDTH, samples), lambda i, elem, reg: (0, 0)),
            pl.BlockSpec((regions, voxels), lambda i, elem, reg: (0, 0)),
        ],
        scratch_shapes=[
            pltpu.VMEM((WIDTH + 2 * SUB, samples), jnp.float32),
            pltpu.VMEM((len(DELTAS), 2 * WIDTH, samples), jnp.bfloat16),
            pltpu.VMEM((16, regions, LANES), jnp.float32),
            pltpu.VMEM((samples, regions), jnp.bfloat16),
            pltpu.VMEM((len(DELTAS), WIDTH, regions), jnp.bfloat16),
            pltpu.VMEM((SUB, WIDTH, regions), jnp.bfloat16),
            pltpu.VMEM((len(WINDOWS), LANES, WIDTH), jnp.bfloat16),
            pltpu.VMEM((len(DELTAS), SUB, WIDTH, regions), jnp.bfloat16),
        ],
    )
    return pl.pallas_call(
        stats_kernel,
        grid_spec=grid_spec,
        out_shape=[
            jax.ShapeDtypeStruct((regions, TILES * LANES), jnp.bfloat16),
            jax.ShapeDtypeStruct((WIDTH, samples), jnp.bfloat16),
            jax.ShapeDtypeStruct((regions, voxels), jnp.int32),
        ],
        compiler_params=pltpu.CompilerParams(vmem_limit_bytes=56 * 1024 * 1024),
        name="stats",
    )(elem, reg, rf, tx_delay, rx_delay, aperture)


def solve_kernel(parts_ref, weights_ref):
    total = jnp.sum(parts_ref[...].astype(jnp.float32), axis=0, keepdims=True)
    tiles = [total[:, t * LANES : (t + 1) * LANES] for t in range(TILES)]
    tall = jnp.concatenate(tiles + [jnp.zeros((LANES - TILES, LANES), jnp.float32)], axis=0)
    turned = jnp.transpose(tall)
    table = jnp.concatenate([turned[0:ORDER, 0:ORDER], turned[ORDER:LANES, 0:ORDER]], axis=1)
    i = row_iota((ORDER, LANES))
    lane = lane_iota((ORDER, LANES))
    j = lane & (ORDER - 1)
    da = ((j // SUB) - (i // SUB)) & (SUB - 1)
    d = ((j & (SUB - 1)) - (i & (SUB - 1))) & (SUB - 1)
    spot = jnp.where(
        d == 1, da,
        jnp.where(
            d == 2, da + ORDER,
            jnp.where(
                d == 3, SUB + (da & 3) + ORDER * (da // 4),
                jnp.where(d == 4, 12 + da, 12 + da + ORDER),
            ),
        ),
    )
    stored = ((d >= 1) & (d <= 3)) | (((d == 0) | (d == 4)) & (da <= 4))
    half = jnp.take_along_axis(table, spot & (LANES - 1), axis=1)
    half = jnp.where(stored & (lane < ORDER), half, 0.0)
    square = jnp.concatenate([half, jnp.zeros((LANES - ORDER, LANES), jnp.float32)], axis=0)
    cov = jnp.where(stored, half, jnp.transpose(square)[0:ORDER, :])
    diagonal = lane == i
    trace = jnp.sum(jnp.sum(jnp.where(diagonal, cov, 0.0), axis=1, keepdims=True), axis=0, keepdims=True)
    cov = cov + jnp.where(diagonal, load_factor * trace / ORDER, 0.0)
    work = jnp.where(lane < ORDER, cov, 1.0)
    column = i[:, 0:1]
    for k in range(ORDER):
        pivot_row = work[k : k + 1, :]
        inverse = 1.0 / pivot_row[:, k : k + 1]
        factor = jnp.where(column == k, 0.0, work[:, k : k + 1] * inverse)
        work = work - factor * pivot_row
    held = jnp.sum(jnp.where(diagonal, work, 0.0), axis=1, keepdims=True)
    solved = work[:, ORDER : ORDER + 1] / held
    row = jnp.sum(jnp.where(diagonal, solved, 0.0), axis=0, keepdims=True)
    weights_ref[...] = row / jnp.sum(row, axis=1, keepdims=True)


def solve(parts):
    return pl.pallas_call(
        solve_kernel,
        out_shape=jax.ShapeDtypeStruct((1, LANES), jnp.float32),
        compiler_params=pltpu.CompilerParams(vmem_limit_bytes=32 * 1024 * 1024),
        name="solve",
    )(parts)


def image_kernel(scale, elem, weights_ref, traces_ref, spots_ref, aperture_ref, out_ref, line_ref):
    regions, voxels = spots_ref.shape
    samples = traces_ref.shape[-1]
    first_row = elem[0] * SUB

    source = row_iota((LANES, WIDTH))
    element = lane_iota((LANES, WIDTH))
    x = source & (SUB - 1)
    k = element & (PROBE - 1)
    spread = (source // SUB == element // PROBE) & (k >= x) & (k <= x + PROBE - SUB)
    spread = spread.astype(jnp.float32).astype(jnp.bfloat16)
    weights = weights_ref[...]
    high, low = split(weights)
    rest = (weights - high.astype(jnp.float32) - low.astype(jnp.float32)).astype(jnp.bfloat16)
    gain = jnp.dot(high, spread, preferred_element_type=jnp.float32)
    gain = gain + jnp.dot(low, spread, preferred_element_type=jnp.float32)
    gain = gain + jnp.dot(rest, spread, preferred_element_type=jnp.float32)
    lane = lane_iota((regions, WIDTH))
    row = lane // PROBE + first_row
    column = lane & (PROBE - 1)
    bounds = aperture_ref[...].astype(jnp.float32)
    bounds = jnp.concatenate([bounds, jnp.zeros((LANES - 4, regions), jnp.float32)], axis=0)
    bounds = jnp.transpose(bounds).astype(jnp.int32)
    inside = (row >= bounds[:, 0:1]) & (row < bounds[:, 1:2])
    inside &= (column >= bounds[:, 2:3]) & (column < bounds[:, 3:4])
    high, low = split(jnp.where(inside, gain * scale, 0.0))
    line_ref[...] = jnp.dot(high, traces_ref[...], preferred_element_type=jnp.float32) + jnp.dot(
        low, traces_ref[...], preferred_element_type=jnp.float32
    )

    sums = spots_ref[...]
    group = 32
    for begin in range(0, regions, group):
        rows = slice(begin, begin + group)
        for v in range(voxels // LANES):
            spots = sums[rows, v * LANES : (v + 1) * LANES]
            fine = spots & (LANES - 1)
            coarse = spots // LANES
            picked = jnp.zeros((group, LANES), jnp.float32)
            for j in range(samples // LANES):
                found = jnp.take_along_axis(line_ref[rows, j * LANES : (j + 1) * LANES], fine, axis=1)
                picked = jnp.where(coarse == j, found, picked)
            out_ref[rows, v * LANES : (v + 1) * LANES] = picked


def image(scale, elem, weights, traces, spots, aperture):
    regions, voxels = spots.shape
    samples = traces.shape[-1]
    grid_spec = pltpu.PrefetchScalarGridSpec(
        num_scalar_prefetch=1,
        grid=(1,),
        in_specs=[
            pl.BlockSpec(weights.shape, lambda i, elem: (0, 0)),
            pl.BlockSpec(traces.shape, lambda i, elem: (0, 0)),
            pl.BlockSpec(spots.shape, lambda i, elem: (0, 0)),
            pl.BlockSpec(aperture.shape, lambda i, elem: (0, 0)),
        ],
        out_specs=pl.BlockSpec((regions, voxels), lambda i, elem: (0, 0)),
        scratch_shapes=[pltpu.VMEM((regions, samples), jnp.float32)],
    )
    return pl.pallas_call(
        functools.partial(image_kernel, scale),
        grid_spec=grid_spec,
        out_shape=jax.ShapeDtypeStruct((regions, voxels), jnp.float32),
        compiler_params=pltpu.CompilerParams(vmem_limit_bytes=32 * 1024 * 1024),
        name="image",
    )(elem, weights, traces, spots, aperture)


BOTH = ("reg", "elem")


def per_device(rf, tx_delay, rx_delay, aperture):
    n_reg = lax.axis_size("reg")
    n_elem = lax.axis_size("elem")
    regions, voxels = rx_delay.shape[0], tx_delay.shape[2]
    devices = n_reg * n_elem
    scale = 8.0 / math.sqrt(n_reg * n_elem * SHIFTS)
    elem = lax.axis_index("elem").astype(jnp.int32).reshape(1)
    reg = lax.axis_index("reg").astype(jnp.int32).reshape(1)
    bounds = aperture.T
    cov, traces, spots = stats(elem, reg, rf, tx_delay, rx_delay, bounds)
    parts = lax.all_to_all(cov, BOTH, 0, 0, tiled=True)
    mine = solve(parts)
    weights = lax.all_to_all(jnp.broadcast_to(mine, (devices, LANES)), BOTH, 0, 0, tiled=True)
    partial = image(scale, elem, weights, traces, spots, bounds)
    owned = partial.reshape(n_reg, regions // n_reg, n_elem, voxels // n_elem).transpose(0, 2, 1, 3)
    owned = owned.reshape(devices, regions // n_reg, voxels // n_elem)
    arrived = lax.all_to_all(owned, BOTH, 0, 0, tiled=True)
    return jnp.sum(arrived, axis=0)


def solution(mesh):
    in_specs = (P("reg", "elem", None), P(), P(None, "elem"), P())
    out_specs = P("reg", "elem")
    return jax.shard_map(
        per_device, mesh=mesh, in_specs=in_specs, out_specs=out_specs, check_vma=False
    )
```

```python
import functools
import math

import jax
import jax.numpy as jnp
from jax import lax
from jax.experimental import pallas as pl
from jax.experimental.pallas import tpu as pltpu
from jax.sharding import PartitionSpec as P

PROBE = 32
SUB = 8
SHIFTS = PROBE - SUB + 1
WIDTH = SUB * PROBE
ORDER = SUB * SUB
LANES = 128

tap_weights = (-0.0625, 0.5625, 0.5625, -0.0625)
load_factor = 0.05

DELTAS = (0, 1, 2, 3, 4, -4, -5, -6, -7)
TILES = 18
WINDOWS = ((1, 0), (-7, 0), (2, 1), (-6, 1), (3, 0), (-5, 0), (3, 1), (-5, 1), (4, 0), (-4, 0), (0, 1))


def lane_iota(shape):
    return lax.broadcasted_iota(jnp.int32, shape, len(shape) - 1)


def row_iota(shape):
    return lax.broadcasted_iota(jnp.int32, shape, 0)


def window_matrix(delta, half):
    element = lane_iota((LANES, WIDTH))
    target = row_iota((LANES, WIDTH)) - ORDER * half
    x = target & (SUB - 1)
    k = element & (PROBE - 1)
    good = (target >= 0) & (target < ORDER)
    good &= (element // PROBE) == (target // SUB)
    good &= (k >= x) & (k <= x + PROBE - SUB)
    good &= (x + delta >= 0) & (x + delta < SUB)
    return good.astype(jnp.float32).astype(jnp.bfloat16)


def split(x):
    high = x.astype(jnp.bfloat16)
    low = (x - high.astype(jnp.float32)).astype(jnp.bfloat16)
    return high, low


def stats_kernel(elem, reg, rf_hbm, tx_hbm, rx_hbm, aperture_hbm, cov_ref, traces_ref, spots_ref,
                 rf_ref, tx_ref, rx_ref, aperture_ref, arrivals,
                 wide, shifted, count32, count16, colmask, rowmask, windows, grams):
    copies = [
        pltpu.make_async_copy(source, target, arrivals.at[which])
        for which, (source, target) in enumerate((
            (rx_hbm, rx_ref),
            (aperture_hbm, aperture_ref),
            (tx_hbm.at[pl.ds(reg[0], 1)], tx_ref),
            (rf_hbm, rf_ref),
        ))
    ]
    for copy in copies:
        copy.start()
    for copy in copies:
        copy.wait()
    regions = rx_ref.shape[0]
    samples = rf_ref.shape[-1]
    blocks = samples // LANES
    voxels = tx_ref.shape[-1]
    first_row = elem[0] * SUB

    rx = rx_ref[...].astype(jnp.float32)
    base = jnp.min(rx, axis=1, keepdims=True)
    lead = rx[0:1, :] - base[0:1, :]
    relative = jnp.transpose(jnp.broadcast_to(lead, (LANES, WIDTH))).astype(jnp.int32)
    wide[0:SUB, :] = jnp.zeros((SUB, samples), jnp.float32)
    wide[SUB + WIDTH : 2 * SUB + WIDTH, :] = jnp.zeros((SUB, samples), jnp.float32)
    step = 32

    def trace_rows(chunk):
        rows = slice(chunk * step, (chunk + 1) * step)
        x = rf_ref[0, rows, :].astype(jnp.float32)
        y = tap_weights[0] * pltpu.roll(x, 1, 1)
        y = y + tap_weights[1] * x
        y = y + tap_weights[2] * pltpu.roll(x, samples - 1, 1)
        y = y + tap_weights[3] * pltpu.roll(x, samples - 2, 1)
        y = y.astype(jnp.bfloat16).astype(jnp.float32)
        move = relative[rows, :]
        fine = move & (LANES - 1)
        reach = lane_iota((step, LANES)) + fine
        spot = reach & (LANES - 1)
        parts = [
            jnp.take_along_axis(y[:, j * LANES : (j + 1) * LANES], spot, axis=1)
            for j in range(blocks)
        ]
        stay = reach < LANES
        parts = [jnp.where(stay, parts[j], parts[(j + 1) % blocks]) for j in range(blocks)]
        for bit in range(3):
            here = (move & (LANES << bit)) != 0
            parts = [
                jnp.where(here, parts[(j + (1 << bit)) % blocks], parts[j]) for j in range(blocks)
            ]
        for j in range(blocks):
            lanes = slice(j * LANES, (j + 1) * LANES)
            wide[SUB + chunk * step : SUB + (chunk + 1) * step, lanes] = parts[j]
            part = parts[j].astype(jnp.bfloat16)
            shifted[0, rows, lanes] = part
            traces_ref[rows, lanes] = part

    def shift_rows(which, chunk):
        begin = SUB + DELTAS[which] + chunk * step
        shifted[which, chunk * step : (chunk + 1) * step, :] = wide[begin : begin + step, :].astype(jnp.bfloat16)

    sums = tx_ref[0] + base.astype(jnp.int32)
    spots_ref[...] = sums
    tall = 16
    packed_rows = row_iota((LANES, voxels)).astype(jnp.float32).astype(jnp.bfloat16)
    one, zero = jnp.ones((), jnp.bfloat16), jnp.zeros((), jnp.bfloat16)
    high_spots = (sums // LANES).astype(jnp.float32)
    low_spots = (sums & (LANES - 1)).astype(jnp.float32)

    def count_region(r):
        high = jnp.broadcast_to(high_spots[r : r + 1, :], (tall, voxels)).astype(jnp.bfloat16)
        low = jnp.broadcast_to(low_spots[r : r + 1, :], (tall, voxels)).astype(jnp.bfloat16)
        low = jnp.concatenate([low] * (LANES // tall), axis=0)
        count32[:, r, :] = lax.dot_general(
            jnp.where(high == packed_rows[0:tall], one, zero),
            jnp.where(low == packed_rows, one, zero),
            (((1,), (1,)), ((), ())),
            preferred_element_type=jnp.float32,
        )

    chunks = WIDTH // step
    for chunk in range(chunks):
        trace_rows(chunk)
        for r in range(chunk * regions // chunks, (chunk + 1) * regions // chunks):
            count_region(r)
    for j in range(blocks):
        count16[j * LANES : (j + 1) * LANES, :] = jnp.transpose(count32[j]).astype(jnp.bfloat16)

    element = row_iota((WIDTH, regions))
    row = element // PROBE
    column = element & (PROBE - 1)
    bounds = aperture_ref[...]
    row_lo, row_hi = bounds[0:1, :] - first_row, bounds[1:2, :] - first_row
    col_lo, col_hi = bounds[2:3, :], bounds[3:4, :]
    column_inside = (column >= col_lo) & (column < col_hi)
    for which, delta in enumerate(DELTAS):
        other = column + delta
        inside = column_inside & (other >= col_lo) & (other < col_hi)
        colmask[which] = inside.astype(jnp.float32).astype(jnp.bfloat16)
    row_inside = (row >= row_lo) & (row < row_hi)
    for da in range(SUB):
        other = (row + da) & (SUB - 1)
        inside = row_inside & (other >= row_lo) & (other < row_hi)
        rowmask[da] = inside.astype(jnp.float32).astype(jnp.bfloat16)

    for slot, (delta, half) in enumerate(WINDOWS):
        windows[slot] = window_matrix(delta, half)

    def gram_terms(which):
        delta = DELTAS[which]
        reach = SUB if delta in (1, 2, 3, -5, -6, -7) else SUB // 2 + 1
        if which:
            for chunk in range(chunks):
                shift_rows(which, chunk)
        pairs = []
        for da in range(reach):
            cut = WIDTH - da * PROBE
            pairs.append(shifted[0, 0:cut, :] * shifted[which, WIDTH - cut : WIDTH, :])
            if da:
                pairs.append(shifted[0, cut:WIDTH, :] * shifted[which, 0 : WIDTH - cut, :])
        gram = jnp.dot(
            jnp.concatenate(pairs, axis=0), count16[...], preferred_element_type=jnp.float32
        ).astype(jnp.bfloat16)
        for da in range(reach):
            grams[which, da] = gram[da * WIDTH : (da + 1) * WIDTH] * colmask[which] * rowmask[da]

    def put(tile, terms):
        left = jnp.concatenate([windows[WINDOWS.index((delta, half))] for delta, half, da in terms], axis=1)
        right = jnp.concatenate([grams[DELTAS.index(delta), da] for delta, half, da in terms], axis=0)
        out = jnp.dot(left, right, preferred_element_type=jnp.float32)
        lane_at = tile % (TILES // 2) * LANES
        cov_ref[tile // (TILES // 2), :, lane_at : lane_at + LANES] = jnp.transpose(out).astype(cov_ref.dtype)

    for delta in (1, -7, 2, -6):
        gram_terms(DELTAS.index(delta))
    gram_terms(DELTAS.index(3))
    for da in range(SUB):
        put(da, ((1, 0, da), (-7, 0, da), (2, 1, da), (-6, 1, da)))
    gram_terms(DELTAS.index(-5))
    gram_terms(DELTAS.index(4))
    for da in range(SUB // 2):
        put(SUB + da, ((3, 0, da), (-5, 0, da), (3, 1, da + 4), (-5, 1, da + 4)))
    gram_terms(DELTAS.index(-4))
    gram_terms(DELTAS.index(0))
    for da in range(SUB // 2 + 1):
        put(12 + da, ((4, 0, da), (-4, 0, da), (0, 1, da)))
    last = (TILES // 2 - 1) * LANES
    cov_ref[1, :, last:] = jnp.zeros((regions, LANES), cov_ref.dtype)


def stats(elem, reg, rf, tx_delay, rx_delay, aperture):
    regions = rx_delay.shape[0]
    samples = rf.shape[-1]
    voxels = tx_delay.shape[-1]
    grid_spec = pltpu.PrefetchScalarGridSpec(
        num_scalar_prefetch=2,
        grid=(1,),
        in_specs=[pl.BlockSpec(memory_space=pltpu.HBM)] * 4,
        out_specs=[
            pl.BlockSpec((2, regions, TILES // 2 * LANES), lambda i, elem, reg: (0, 0, 0)),
            pl.BlockSpec((WIDTH, samples), lambda i, elem, reg: (0, 0)),
            pl.BlockSpec((regions, voxels), lambda i, elem, reg: (0, 0)),
        ],
        scratch_shapes=[
            pltpu.VMEM(rf.shape, rf.dtype),
            pltpu.VMEM((1, regions, voxels), tx_delay.dtype),
            pltpu.VMEM(rx_delay.shape, rx_delay.dtype),
            pltpu.VMEM(aperture.shape, aperture.dtype),
            pltpu.SemaphoreType.DMA((4,)),
            pltpu.VMEM((WIDTH + 2 * SUB, samples), jnp.float32),
            pltpu.VMEM((len(DELTAS), WIDTH, samples), jnp.bfloat16),
            pltpu.VMEM((16, regions, LANES), jnp.float32),
            pltpu.VMEM((samples, regions), jnp.bfloat16),
            pltpu.VMEM((len(DELTAS), WIDTH, regions), jnp.bfloat16),
            pltpu.VMEM((SUB, WIDTH, regions), jnp.bfloat16),
            pltpu.VMEM((len(WINDOWS), LANES, WIDTH), jnp.bfloat16),
            pltpu.VMEM((len(DELTAS), SUB, WIDTH, regions), jnp.bfloat16),
        ],
    )
    return pl.pallas_call(
        stats_kernel,
        grid_spec=grid_spec,
        out_shape=[
            jax.ShapeDtypeStruct((2, regions, TILES // 2 * LANES), jnp.bfloat16),
            jax.ShapeDtypeStruct((WIDTH, samples), jnp.bfloat16),
            jax.ShapeDtypeStruct((regions, voxels), jnp.int32),
        ],
        compiler_params=pltpu.CompilerParams(vmem_limit_bytes=44 * 1024 * 1024),
        name="stats",
    )(elem, reg, rf, tx_delay, rx_delay, aperture)


def solve_kernel(total_ref, weights_ref):
    total = total_ref[...]
    per = TILES // 2
    tiles = [total[t // per : t // per + 1, t % per * LANES : (t % per + 1) * LANES] for t in range(TILES)]
    tall = jnp.concatenate(tiles + [jnp.zeros((LANES - TILES, LANES), jnp.float32)], axis=0)
    turned = jnp.transpose(tall)
    table = jnp.concatenate([turned[0:ORDER, 0:ORDER], turned[ORDER:LANES, 0:ORDER]], axis=1)
    i = row_iota((ORDER, LANES))
    lane = lane_iota((ORDER, LANES))
    j = lane & (ORDER - 1)
    da = ((j // SUB) - (i // SUB)) & (SUB - 1)
    d = ((j & (SUB - 1)) - (i & (SUB - 1))) & (SUB - 1)
    spot = jnp.where(
        d == 1, da,
        jnp.where(
            d == 2, da + ORDER,
            jnp.where(
                d == 3, SUB + (da & 3) + ORDER * (da // 4),
                jnp.where(d == 4, 12 + da, 12 + da + ORDER),
            ),
        ),
    )
    stored = ((d >= 1) & (d <= 3)) | (((d == 0) | (d == 4)) & (da <= 4))
    half = jnp.take_along_axis(table, spot & (LANES - 1), axis=1)
    half = jnp.where(stored & (lane < ORDER), half, 0.0)
    square = jnp.concatenate([half, jnp.zeros((LANES - ORDER, LANES), jnp.float32)], axis=0)
    cov = jnp.where(stored, half, jnp.transpose(square)[0:ORDER, :])
    diagonal = lane == i
    trace = jnp.sum(jnp.sum(jnp.where(diagonal, cov, 0.0), axis=1, keepdims=True), axis=0, keepdims=True)
    cov = cov + jnp.where(diagonal, load_factor * trace / ORDER, 0.0)
    work = jnp.where(lane < ORDER, cov, 1.0)
    high = 8
    shape = (high, LANES)
    sublane = row_iota(shape)
    groups = [work[g : g + high, :] for g in range(0, ORDER, high)]
    def spread(part, k):
        return jnp.broadcast_to(part[:, k : k + 1], shape)

    for k in range(0, ORDER, 4):
        at, inner = k // high, k % high
        rows = [jnp.broadcast_to(groups[at][inner + n : inner + n + 1, :], shape) for n in range(4)]
        m = [[spread(rows[n], k + c) for c in range(4)] for n in range(4)]
        inverse = 1.0 / (m[0][0] * m[1][1] - m[0][1] * m[1][0])
        i00, i01 = m[1][1] * inverse, -m[0][1] * inverse
        i10, i11 = -m[1][0] * inverse, m[0][0] * inverse
        e02, e03 = i00 * m[0][2] + i01 * m[1][2], i00 * m[0][3] + i01 * m[1][3]
        e12, e13 = i10 * m[0][2] + i11 * m[1][2], i10 * m[0][3] + i11 * m[1][3]
        first = i00 * rows[0] + i01 * rows[1]
        second = i10 * rows[0] + i11 * rows[1]
        third = rows[2] - m[2][0] * first - m[2][1] * second
        fourth = rows[3] - m[3][0] * first - m[3][1] * second
        s22 = m[2][2] - m[2][0] * e02 - m[2][1] * e12
        s23 = m[2][3] - m[2][0] * e03 - m[2][1] * e13
        s32 = m[3][2] - m[3][0] * e02 - m[3][1] * e12
        s33 = m[3][3] - m[3][0] * e03 - m[3][1] * e13
        inverse = 1.0 / (s22 * s33 - s23 * s32)
        third, fourth = (third * s33 - fourth * s23) * inverse, (fourth * s22 - third * s32) * inverse
        first = first - e02 * third - e03 * fourth
        second = second - e12 * third - e13 * fourth
        solved_rows = (first, second, third, fourth)
        updated = []
        for g, part in enumerate(groups):
            change = sum(spread(part, k + c) * solved_rows[c] for c in range(4))
            new = part - change
            if g == at:
                for c in range(4):
                    new = jnp.where(sublane == inner + c, solved_rows[c], new)
            updated.append(new)
        groups = updated
    solved = jnp.concatenate(groups, axis=0)[:, ORDER : ORDER + 1]
    row = jnp.sum(jnp.where(diagonal, solved, 0.0), axis=0, keepdims=True)
    weights_ref[...] = row / jnp.sum(row, axis=1, keepdims=True)


def solve(parts):
    return pl.pallas_call(
        solve_kernel,
        out_shape=jax.ShapeDtypeStruct((1, LANES), jnp.float32),
        compiler_params=pltpu.CompilerParams(vmem_limit_bytes=32 * 1024 * 1024),
        name="solve",
    )(parts)


def image_kernel(scale, elem, weights_ref, traces_ref, spots_ref, aperture_ref, out_ref, line_ref):
    regions, voxels = spots_ref.shape
    samples = traces_ref.shape[-1]
    first_row = elem[0] * SUB

    source = row_iota((LANES, WIDTH))
    element = lane_iota((LANES, WIDTH))
    x = source & (SUB - 1)
    k = element & (PROBE - 1)
    spread = (source // SUB == element // PROBE) & (k >= x) & (k <= x + PROBE - SUB)
    spread = spread.astype(jnp.float32).astype(jnp.bfloat16)
    weights = weights_ref[...]
    high, low = split(weights)
    gain = jnp.dot(high, spread, preferred_element_type=jnp.float32)
    gain = gain + jnp.dot(low, spread, preferred_element_type=jnp.float32)
    lane = lane_iota((regions, WIDTH))
    row = lane // PROBE + first_row
    column = lane & (PROBE - 1)
    bounds = aperture_ref[...].astype(jnp.float32)
    bounds = jnp.concatenate([bounds, jnp.zeros((LANES - 4, regions), jnp.float32)], axis=0)
    bounds = jnp.transpose(bounds).astype(jnp.int32)
    inside = (row >= bounds[:, 0:1]) & (row < bounds[:, 1:2])
    inside &= (column >= bounds[:, 2:3]) & (column < bounds[:, 3:4])
    high, low = split(jnp.where(inside, gain * scale, 0.0))
    line_ref[...] = jnp.dot(high, traces_ref[...], preferred_element_type=jnp.float32) + jnp.dot(
        low, traces_ref[...], preferred_element_type=jnp.float32
    )

    sums = spots_ref[...]
    group = 32
    for begin in range(0, regions, group):
        rows = slice(begin, begin + group)
        for v in range(voxels // LANES):
            spots = sums[rows, v * LANES : (v + 1) * LANES]
            fine = spots & (LANES - 1)
            coarse = spots // LANES
            picked = jnp.zeros((group, LANES), jnp.float32)
            for j in range(samples // LANES):
                found = jnp.take_along_axis(line_ref[rows, j * LANES : (j + 1) * LANES], fine, axis=1)
                picked = jnp.where(coarse == j, found, picked)
            out_ref[rows, v * LANES : (v + 1) * LANES] = picked


def image(scale, elem, weights, traces, spots, aperture):
    regions, voxels = spots.shape
    samples = traces.shape[-1]
    grid_spec = pltpu.PrefetchScalarGridSpec(
        num_scalar_prefetch=1,
        grid=(1,),
        in_specs=[
            pl.BlockSpec(weights.shape, lambda i, elem: (0, 0)),
            pl.BlockSpec(traces.shape, lambda i, elem: (0, 0)),
            pl.BlockSpec(spots.shape, lambda i, elem: (0, 0)),
            pl.BlockSpec(aperture.shape, lambda i, elem: (0, 0)),
        ],
        out_specs=pl.BlockSpec((regions, voxels), lambda i, elem: (0, 0)),
        scratch_shapes=[pltpu.VMEM((regions, samples), jnp.float32)],
    )
    return pl.pallas_call(
        functools.partial(image_kernel, scale),
        grid_spec=grid_spec,
        out_shape=jax.ShapeDtypeStruct((regions, voxels), jnp.float32),
        compiler_params=pltpu.CompilerParams(vmem_limit_bytes=32 * 1024 * 1024),
        name="image",
    )(elem, weights, traces, spots, aperture)


BOTH = ("reg", "elem")


def per_device(rf, tx_delay, rx_delay, aperture):
    n_reg = lax.axis_size("reg")
    n_elem = lax.axis_size("elem")
    regions, voxels = rx_delay.shape[0], tx_delay.shape[2]
    devices = n_reg * n_elem
    scale = 8.0 / math.sqrt(n_reg * n_elem * SHIFTS)
    elem = lax.axis_index("elem").astype(jnp.int32).reshape(1)
    reg = lax.axis_index("reg").astype(jnp.int32).reshape(1)
    bounds = aperture.T
    cov, traces, spots = stats(elem, reg, rf, tx_delay, rx_delay, bounds)
    parts = lax.all_to_all(cov.transpose(1, 0, 2), BOTH, 0, 0, tiled=True)
    mine = solve(jnp.sum(parts.astype(jnp.float32), axis=0))
    weights = lax.all_to_all(jnp.broadcast_to(mine, (devices, LANES)), BOTH, 0, 0, tiled=True)
    partial = image(scale, elem, weights, traces, spots, bounds)
    owned = partial.reshape(n_reg, regions // n_reg, n_elem, voxels // n_elem).transpose(0, 2, 1, 3)
    owned = owned.reshape(devices, regions // n_reg, voxels // n_elem)
    arrived = lax.all_to_all(owned, BOTH, 0, 0, tiled=True)
    return jnp.sum(arrived, axis=0)


def solution(mesh):
    in_specs = (P("reg", "elem", None), P(), P(None, "elem"), P())
    out_specs = P("reg", "elem")
    return jax.shard_map(
        per_device, mesh=mesh, in_specs=in_specs, out_specs=out_specs, check_vma=False
    )
```

```python
import functools
import math

import jax
import jax.numpy as jnp
from jax import lax
from jax.experimental import pallas as pl
from jax.experimental.pallas import tpu as pltpu
from jax.sharding import PartitionSpec as P

PROBE = 32
SUB = 8
SHIFTS = PROBE - SUB + 1
WIDTH = SUB * PROBE
ORDER = SUB * SUB
LANES = 128

tap_weights = (-0.0625, 0.5625, 0.5625, -0.0625)
load_factor = 0.05

DELTAS = (0, 1, 2, 3, 4, -4, -5, -6, -7)
TILES = 18
WINDOWS = ((1, 0), (-7, 0), (2, 1), (-6, 1), (3, 0), (-5, 0), (3, 1), (-5, 1), (4, 0), (-4, 0), (0, 1))


def lane_iota(shape):
    return lax.broadcasted_iota(jnp.int32, shape, len(shape) - 1)


def row_iota(shape):
    return lax.broadcasted_iota(jnp.int32, shape, 0)


def window_matrix(delta, half):
    element = lane_iota((LANES, WIDTH))
    target = row_iota((LANES, WIDTH)) - ORDER * half
    x = target & (SUB - 1)
    k = element & (PROBE - 1)
    good = (target >= 0) & (target < ORDER)
    good &= (element // PROBE) == (target // SUB)
    good &= (k >= x) & (k <= x + PROBE - SUB)
    good &= (x + delta >= 0) & (x + delta < SUB)
    return good.astype(jnp.float32).astype(jnp.bfloat16)


def split(x):
    high = x.astype(jnp.bfloat16)
    low = (x - high.astype(jnp.float32)).astype(jnp.bfloat16)
    return high, low


def stats_kernel(elem, reg, rf_ref, tx_hbm, rx_ref, aperture_ref, keep_ref, send_ref, traces_ref, spots_ref,
                 tx_ref, arrival,
                 wide, shifted, count32, count16, colmask, rowmask, windows, grams):
    tx_copy = pltpu.make_async_copy(tx_hbm.at[pl.ds(reg[0], 1)], tx_ref, arrival)
    tx_copy.start()
    core = reg[0] & 1
    regions = rx_ref.shape[0]
    samples = rf_ref.shape[-1]
    blocks = samples // LANES
    voxels = tx_ref.shape[-1]
    first_row = elem[0] * SUB

    rx = rx_ref[...].astype(jnp.float32)
    base = jnp.min(rx, axis=1, keepdims=True)
    lead = rx[0:1, :] - base[0:1, :]
    relative = jnp.transpose(jnp.broadcast_to(lead, (LANES, WIDTH))).astype(jnp.int32)
    wide[0:SUB, :] = jnp.zeros((SUB, samples), jnp.float32)
    wide[SUB + WIDTH : 2 * SUB + WIDTH, :] = jnp.zeros((SUB, samples), jnp.float32)
    step = 32

    def trace_rows(chunk):
        rows = slice(chunk * step, (chunk + 1) * step)
        x = rf_ref[0, rows, :].astype(jnp.float32)
        y = tap_weights[0] * pltpu.roll(x, 1, 1)
        y = y + tap_weights[1] * x
        y = y + tap_weights[2] * pltpu.roll(x, samples - 1, 1)
        y = y + tap_weights[3] * pltpu.roll(x, samples - 2, 1)
        y = y.astype(jnp.bfloat16).astype(jnp.float32)
        move = relative[rows, :]
        fine = move & (LANES - 1)
        reach = lane_iota((step, LANES)) + fine
        spot = reach & (LANES - 1)
        parts = [
            jnp.take_along_axis(y[:, j * LANES : (j + 1) * LANES], spot, axis=1)
            for j in range(blocks)
        ]
        stay = reach < LANES
        parts = [jnp.where(stay, parts[j], parts[(j + 1) % blocks]) for j in range(blocks)]
        for bit in range(3):
            here = (move & (LANES << bit)) != 0
            parts = [
                jnp.where(here, parts[(j + (1 << bit)) % blocks], parts[j]) for j in range(blocks)
            ]
        for j in range(blocks):
            lanes = slice(j * LANES, (j + 1) * LANES)
            wide[SUB + chunk * step : SUB + (chunk + 1) * step, lanes] = parts[j]
            part = parts[j].astype(jnp.bfloat16)
            shifted[0, rows, lanes] = part
            traces_ref[rows, lanes] = part

    def shift_rows(which, chunk):
        begin = SUB + DELTAS[which] + chunk * step
        shifted[which, chunk * step : (chunk + 1) * step, :] = wide[begin : begin + step, :].astype(jnp.bfloat16)

    trace_rows(0)
    tx_copy.wait()

    sums = tx_ref[0] + base.astype(jnp.int32)
    spots_ref[...] = sums
    tall, fine_bins = 16, 64
    coarse_bins = samples // fine_bins
    packed_rows = row_iota((fine_bins, voxels)).astype(jnp.float32).astype(jnp.bfloat16)
    one, zero = jnp.ones((), jnp.bfloat16), jnp.zeros((), jnp.bfloat16)
    coarse_spots = (sums // fine_bins).astype(jnp.float32)
    fine_spots = (sums & (fine_bins - 1)).astype(jnp.float32)

    def one_hot(spots, r, bins):
        line = jnp.broadcast_to(spots[r : r + 1, :], (tall, voxels)).astype(jnp.bfloat16)
        line = jnp.concatenate([line] * (bins // tall), axis=0)
        return jnp.where(line == packed_rows[0:bins], one, zero)

    def count_region(r):
        at = (r // 4 % 2 * (regions // 2) + r // 8 * 4 + r % 4) * coarse_bins
        count32[at : at + coarse_bins, :] = lax.dot_general(
            one_hot(coarse_spots, r, coarse_bins),
            one_hot(fine_spots, r, fine_bins),
            (((1,), (1,)), ((), ())),
            preferred_element_type=jnp.float32,
        )

    chunks = WIDTH // step
    for chunk in range(chunks):
        if chunk:
            trace_rows(chunk)
        for r in range(chunk * regions // chunks, (chunk + 1) * regions // chunks):
            count_region(r)
    for j in range(blocks):
        both = [count32[pl.ds(2 * j + q, regions, stride=coarse_bins), :] for q in range(2)]
        count16[j * LANES : (j + 1) * LANES, :] = jnp.transpose(
            jnp.concatenate(both, axis=1)
        ).astype(jnp.bfloat16)

    element = row_iota((WIDTH, regions))
    row = element // PROBE
    column = element & (PROBE - 1)
    place = lane_iota((8, regions))
    place = place % (regions // 2) // 4 * 8 + place // (regions // 2) * 4 + place % 4
    bounds = jnp.concatenate([aperture_ref[...], jnp.zeros((4, regions), jnp.int32)], axis=0)
    bounds = jnp.take_along_axis(bounds, place, axis=1)
    row_lo, row_hi = bounds[0:1, :] - first_row, bounds[1:2, :] - first_row
    col_lo, col_hi = bounds[2:3, :], bounds[3:4, :]
    column_inside = (column >= col_lo) & (column < col_hi)
    for which, delta in enumerate(DELTAS):
        other = column + delta
        inside = column_inside & (other >= col_lo) & (other < col_hi)
        colmask[which] = inside.astype(jnp.float32).astype(jnp.bfloat16)
    row_inside = (row >= row_lo) & (row < row_hi)
    for da in range(SUB):
        other = (row + da) & (SUB - 1)
        inside = row_inside & (other >= row_lo) & (other < row_hi)
        rowmask[da] = inside.astype(jnp.float32).astype(jnp.bfloat16)

    for slot, (delta, half) in enumerate(WINDOWS):
        windows[slot] = window_matrix(delta, half)

    def gram_terms(which):
        delta = DELTAS[which]
        reach = SUB if delta in (1, 2, 3, -5, -6, -7) else SUB // 2 + 1
        if which:
            for chunk in range(chunks):
                shift_rows(which, chunk)
        pairs = []
        for da in range(reach):
            cut = WIDTH - da * PROBE
            pairs.append(shifted[0, 0:cut, :] * shifted[which, WIDTH - cut : WIDTH, :])
            if da:
                pairs.append(shifted[0, cut:WIDTH, :] * shifted[which, 0 : WIDTH - cut, :])
        gram = jnp.dot(
            jnp.concatenate(pairs, axis=0), count16[...], preferred_element_type=jnp.float32
        ).astype(jnp.bfloat16)
        for da in range(reach):
            grams[which, da] = gram[da * WIDTH : (da + 1) * WIDTH] * colmask[which] * rowmask[da]

    def put(tile, terms):
        left = jnp.concatenate([windows[WINDOWS.index((delta, half))] for delta, half, da in terms], axis=1)
        right = jnp.concatenate([grams[DELTAS.index(delta), da] for delta, half, da in terms], axis=0)
        out = jnp.dot(left, right, preferred_element_type=jnp.float32)
        out = jnp.transpose(out).astype(jnp.bfloat16)
        top, bottom = out[: regions // 2], out[regions // 2 :]
        at = (tile // (TILES // 2), slice(None), pl.ds(tile % (TILES // 2) * LANES, LANES))
        keep_ref[at] = jnp.where(core == 0, top, bottom)
        send_ref[at] = jnp.where(core == 0, bottom, top)

    for delta in (1, -7, 2, -6):
        gram_terms(DELTAS.index(delta))
    gram_terms(DELTAS.index(3))
    for da in range(SUB):
        put(da, ((1, 0, da), (-7, 0, da), (2, 1, da), (-6, 1, da)))
    gram_terms(DELTAS.index(-5))
    gram_terms(DELTAS.index(4))
    for da in range(SUB // 2):
        put(SUB + da, ((3, 0, da), (-5, 0, da), (3, 1, da + 4), (-5, 1, da + 4)))
    gram_terms(DELTAS.index(-4))
    gram_terms(DELTAS.index(0))
    for da in range(SUB // 2 + 1):
        put(12 + da, ((4, 0, da), (-4, 0, da), (0, 1, da)))
    last = (TILES // 2 - 1) * LANES
    for ref in (keep_ref, send_ref):
        ref[1, :, last:] = jnp.zeros((regions // 2, LANES), ref.dtype)


def stats(elem, reg, rf, tx_delay, rx_delay, aperture):
    regions = rx_delay.shape[0]
    samples = rf.shape[-1]
    voxels = tx_delay.shape[-1]
    vmem = pl.BlockSpec(memory_space=pltpu.VMEM)
    smem = pl.BlockSpec(memory_space=pltpu.SMEM)
    share = jax.ShapeDtypeStruct((2, regions // 2, TILES // 2 * LANES), jnp.bfloat16)
    return pl.pallas_call(
        stats_kernel,
        in_specs=[smem, smem, vmem, pl.BlockSpec(memory_space=pltpu.HBM), vmem, vmem],
        out_specs=[vmem] * 4,
        out_shape=[
            share,
            share,
            jax.ShapeDtypeStruct((WIDTH, samples), jnp.bfloat16),
            jax.ShapeDtypeStruct((regions, voxels), jnp.int32),
        ],
        scratch_shapes=[
            pltpu.VMEM((1, regions, voxels), tx_delay.dtype),
            pltpu.SemaphoreType.DMA,
            pltpu.VMEM((WIDTH + 2 * SUB, samples), jnp.float32),
            pltpu.VMEM((len(DELTAS), WIDTH, samples), jnp.bfloat16),
            pltpu.VMEM((samples // 64 * regions, 64), jnp.float32),
            pltpu.VMEM((samples, regions), jnp.bfloat16),
            pltpu.VMEM((len(DELTAS), WIDTH, regions), jnp.bfloat16),
            pltpu.VMEM((SUB, WIDTH, regions), jnp.bfloat16),
            pltpu.VMEM((len(WINDOWS), LANES, WIDTH), jnp.bfloat16),
            pltpu.VMEM((len(DELTAS), SUB, WIDTH, regions), jnp.bfloat16),
        ],
        compiler_params=pltpu.CompilerParams(vmem_limit_bytes=44 * 1024 * 1024),
        name="stats",
    )(elem, reg, rf, tx_delay, rx_delay, aperture)


def solve_kernel(total_ref, weights_ref):
    total = total_ref[...]
    per = TILES // 2
    tiles = [total[t // per : t // per + 1, t % per * LANES : (t % per + 1) * LANES] for t in range(TILES)]
    tall = jnp.concatenate(tiles + [jnp.zeros((LANES - TILES, LANES), jnp.float32)], axis=0)
    turned = jnp.transpose(tall)
    table = jnp.concatenate([turned[0:ORDER, 0:ORDER], turned[ORDER:LANES, 0:ORDER]], axis=1)
    i = row_iota((ORDER, LANES))
    lane = lane_iota((ORDER, LANES))
    j = lane & (ORDER - 1)
    da = ((j // SUB) - (i // SUB)) & (SUB - 1)
    d = ((j & (SUB - 1)) - (i & (SUB - 1))) & (SUB - 1)
    spot = jnp.where(
        d == 1, da,
        jnp.where(
            d == 2, da + ORDER,
            jnp.where(
                d == 3, SUB + (da & 3) + ORDER * (da // 4),
                jnp.where(d == 4, 12 + da, 12 + da + ORDER),
            ),
        ),
    )
    stored = ((d >= 1) & (d <= 3)) | (((d == 0) | (d == 4)) & (da <= 4))
    half = jnp.take_along_axis(table, spot & (LANES - 1), axis=1)
    half = jnp.where(stored & (lane < ORDER), half, 0.0)
    square = jnp.concatenate([half, jnp.zeros((LANES - ORDER, LANES), jnp.float32)], axis=0)
    cov = jnp.where(stored, half, jnp.transpose(square)[0:ORDER, :])
    diagonal = lane == i
    trace = jnp.sum(jnp.sum(jnp.where(diagonal, cov, 0.0), axis=1, keepdims=True), axis=0, keepdims=True)
    cov = cov + jnp.where(diagonal, load_factor * trace / ORDER, 0.0)
    work = jnp.where(lane < ORDER, cov, 1.0)
    high = 8
    shape = (high, LANES)
    sublane = row_iota(shape)
    groups = [work[g : g + high, :] for g in range(0, ORDER, high)]
    def spread(part, k):
        return jnp.broadcast_to(part[:, k : k + 1], shape)

    for k in range(0, ORDER, 4):
        at, inner = k // high, k % high
        rows = [jnp.broadcast_to(groups[at][inner + n : inner + n + 1, :], shape) for n in range(4)]
        m = [[spread(rows[n], k + c) for c in range(4)] for n in range(4)]
        inverse = 1.0 / (m[0][0] * m[1][1] - m[0][1] * m[1][0])
        i00, i01 = m[1][1] * inverse, -m[0][1] * inverse
        i10, i11 = -m[1][0] * inverse, m[0][0] * inverse
        e02, e03 = i00 * m[0][2] + i01 * m[1][2], i00 * m[0][3] + i01 * m[1][3]
        e12, e13 = i10 * m[0][2] + i11 * m[1][2], i10 * m[0][3] + i11 * m[1][3]
        first = i00 * rows[0] + i01 * rows[1]
        second = i10 * rows[0] + i11 * rows[1]
        third = rows[2] - m[2][0] * first - m[2][1] * second
        fourth = rows[3] - m[3][0] * first - m[3][1] * second
        s22 = m[2][2] - m[2][0] * e02 - m[2][1] * e12
        s23 = m[2][3] - m[2][0] * e03 - m[2][1] * e13
        s32 = m[3][2] - m[3][0] * e02 - m[3][1] * e12
        s33 = m[3][3] - m[3][0] * e03 - m[3][1] * e13
        inverse = 1.0 / (s22 * s33 - s23 * s32)
        third, fourth = (third * s33 - fourth * s23) * inverse, (fourth * s22 - third * s32) * inverse
        first = first - e02 * third - e03 * fourth
        second = second - e12 * third - e13 * fourth
        solved_rows = (first, second, third, fourth)
        updated = []
        for g, part in enumerate(groups):
            change = sum(spread(part, k + c) * solved_rows[c] for c in range(4))
            new = part - change
            if g == at:
                for c in range(4):
                    new = jnp.where(sublane == inner + c, solved_rows[c], new)
            updated.append(new)
        groups = updated
    solved = jnp.concatenate(groups, axis=0)[:, ORDER : ORDER + 1]
    row = jnp.sum(jnp.where(diagonal, solved, 0.0), axis=0, keepdims=True)
    weights_ref[...] = row / jnp.sum(row, axis=1, keepdims=True)


def solve(parts):
    return pl.pallas_call(
        solve_kernel,
        out_shape=jax.ShapeDtypeStruct((1, LANES), jnp.float32),
        compiler_params=pltpu.CompilerParams(vmem_limit_bytes=32 * 1024 * 1024),
        name="solve",
    )(parts)


def image_kernel(scale, elem, weights_ref, traces_ref, spots_ref, aperture_ref, out_ref, line_ref):
    regions, voxels = spots_ref.shape
    samples = traces_ref.shape[-1]
    first_row = elem[0] * SUB

    source = row_iota((LANES, WIDTH))
    element = lane_iota((LANES, WIDTH))
    x = source & (SUB - 1)
    k = element & (PROBE - 1)
    spread = (source // SUB == element // PROBE) & (k >= x) & (k <= x + PROBE - SUB)
    spread = spread.astype(jnp.float32).astype(jnp.bfloat16)
    weights = weights_ref[...]
    high, low = split(weights)
    gain = jnp.dot(high, spread, preferred_element_type=jnp.float32)
    gain = gain + jnp.dot(low, spread, preferred_element_type=jnp.float32)
    lane = lane_iota((regions, WIDTH))
    row = lane // PROBE + first_row
    column = lane & (PROBE - 1)
    bounds = aperture_ref[...].astype(jnp.float32)
    bounds = jnp.concatenate([bounds, jnp.zeros((LANES - 4, regions), jnp.float32)], axis=0)
    bounds = jnp.transpose(bounds).astype(jnp.int32)
    inside = (row >= bounds[:, 0:1]) & (row < bounds[:, 1:2])
    inside &= (column >= bounds[:, 2:3]) & (column < bounds[:, 3:4])
    high, low = split(jnp.where(inside, gain * scale, 0.0))
    both = jnp.dot(
        jnp.concatenate([high, low], axis=0), traces_ref[...], preferred_element_type=jnp.float32
    )
    line_ref[...] = both[:regions] + both[regions:]

    sums = spots_ref[...]
    group = 32
    for begin in range(0, regions, group):
        rows = slice(begin, begin + group)
        for v in range(voxels // LANES):
            spots = sums[rows, v * LANES : (v + 1) * LANES]
            fine = spots & (LANES - 1)
            coarse = spots // LANES
            picked = jnp.zeros((group, LANES), jnp.float32)
            for j in range(samples // LANES):
                found = jnp.take_along_axis(line_ref[rows, j * LANES : (j + 1) * LANES], fine, axis=1)
                picked = jnp.where(coarse == j, found, picked)
            out_ref[rows, v * LANES : (v + 1) * LANES] = picked


def image(scale, elem, weights, traces, spots, aperture):
    regions, voxels = spots.shape
    samples = traces.shape[-1]
    vmem = pl.BlockSpec(memory_space=pltpu.VMEM)
    return pl.pallas_call(
        functools.partial(image_kernel, scale),
        in_specs=[pl.BlockSpec(memory_space=pltpu.SMEM), vmem, vmem, vmem, vmem],
        out_specs=vmem,
        out_shape=jax.ShapeDtypeStruct((regions, voxels), jnp.float32),
        scratch_shapes=[pltpu.VMEM((regions, samples), jnp.float32)],
        compiler_params=pltpu.CompilerParams(vmem_limit_bytes=32 * 1024 * 1024),
        name="image",
    )(elem, weights, traces, spots, aperture)


REG = ("xy", "core")
BOTH = ("xy", "core", "elem")
CHIPS = ("xy", "elem")


def per_device(rf, tx_delay, rx_delay, aperture):
    n_reg = lax.axis_size("xy") * lax.axis_size("core")
    n_elem = lax.axis_size("elem")
    regions, voxels = rx_delay.shape[0], tx_delay.shape[2]
    devices = n_reg * n_elem
    scale = 8.0 / math.sqrt(n_reg * n_elem * SHIFTS)
    elem = lax.axis_index("elem").astype(jnp.int32).reshape(1)
    reg = lax.axis_index(REG).astype(jnp.int32).reshape(1)
    bounds = aperture.T
    keep, send, traces, spots = stats(elem, reg, rf, tx_delay, rx_delay, bounds)
    other = lax.ppermute(send, "core", [(0, 1), (1, 0)])
    chip = (keep.astype(jnp.float32) + other.astype(jnp.float32)).astype(jnp.bfloat16)
    parts = lax.all_to_all(chip.transpose(1, 0, 2), CHIPS, 0, 0, tiled=True)
    mine = solve(jnp.sum(parts.astype(jnp.float32), axis=0))
    weights = lax.all_to_all(jnp.broadcast_to(mine, (devices, LANES)), BOTH, 0, 0, tiled=True)
    partial = image(scale, elem, weights, traces, spots, bounds)
    owned = partial.reshape(n_reg, regions // n_reg, n_elem, voxels // n_elem).transpose(0, 2, 1, 3)
    owned = owned.reshape(devices, regions // n_reg, voxels // n_elem)
    arrived = lax.all_to_all(owned, BOTH, 0, 0, tiled=True)
    return jnp.sum(arrived, axis=0)


def solution(mesh):
    n_elem, n_reg = mesh.shape["elem"], mesh.shape["reg"]
    chips = jax.sharding.Mesh(mesh.devices.reshape(n_elem, n_reg // 2, 2), ("elem", "xy", "core"))
    in_specs = (P(REG, "elem", None), P(), P(None, "elem"), P())
    out_specs = P(REG, "elem")
    return jax.shard_map(
        per_device, mesh=chips, in_specs=in_specs, out_specs=out_specs, check_vma=False
    )
```

```python
import functools
import math

import jax
import jax.numpy as jnp
from jax import lax
from jax.experimental import pallas as pl
from jax.experimental.pallas import tpu as pltpu
from jax.sharding import PartitionSpec as P

PROBE = 32
SUB = 8
SHIFTS = PROBE - SUB + 1
WIDTH = SUB * PROBE
ORDER = SUB * SUB
LANES = 128

tap_weights = (-0.0625, 0.5625, 0.5625, -0.0625)
load_factor = 0.05

DELTAS = (0, 1, 2, 3, 4, -5, -6, -7)
TILES = 18
WINDOWS = (
    (1, 0, 0), (-7, 0, 0), (2, 1, 0), (-6, 1, 0), (3, 0, 0), (-5, 0, 0), (3, 1, 0), (-5, 1, 0),
    (4, 0, 0), (4, 0, 4), (4, 0, 5), (4, 0, 6), (4, 0, 7), (0, 1, 0), (0, 0, 0),
)


def lane_iota(shape):
    return lax.broadcasted_iota(jnp.int32, shape, len(shape) - 1)


def row_iota(shape):
    return lax.broadcasted_iota(jnp.int32, shape, 0)


def window_matrix(delta, half, turn):
    element = lane_iota((LANES, WIDTH))
    target = row_iota((LANES, WIDTH)) - ORDER * half
    x = target & (SUB - 1)
    k = element & (PROBE - 1)
    good = (target >= 0) & (target < ORDER)
    if turn:
        x = x - 4
        good &= x >= 0
    good &= ((element // PROBE + turn) & (SUB - 1)) == (target // SUB)
    good &= (k >= x) & (k <= x + PROBE - SUB)
    good &= (x + delta >= 0) & (x + delta < SUB)
    return good.astype(jnp.float32).astype(jnp.bfloat16)


def split(x):
    high = x.astype(jnp.bfloat16)
    low = (x - high.astype(jnp.float32)).astype(jnp.bfloat16)
    return high, low


def stats_kernel(elem, reg, rf_ref, tx_hbm, rx_ref, aperture_ref, keep_ref, send_ref, traces_ref, spots_ref,
                 tx_ref, arrival,
                 wide, shifted, count32, count16, colmask, rowmask, windows, grams):
    tx_copy = pltpu.make_async_copy(tx_hbm.at[pl.ds(reg[0], 1)], tx_ref, arrival)
    tx_copy.start()
    core = reg[0] & 1
    regions = rx_ref.shape[0]
    samples = rf_ref.shape[-1]
    blocks = samples // LANES
    voxels = tx_ref.shape[-1]
    first_row = elem[0] * SUB

    rx = rx_ref[...].astype(jnp.float32)
    base = jnp.min(rx, axis=1, keepdims=True)
    lead = rx[0:1, :] - base[0:1, :]
    relative = jnp.transpose(jnp.broadcast_to(lead, (LANES, WIDTH))).astype(jnp.int32)
    wide[0:SUB, :] = jnp.zeros((SUB, samples), jnp.float32)
    wide[SUB + WIDTH : 2 * SUB + WIDTH, :] = jnp.zeros((SUB, samples), jnp.float32)
    step = 32

    def trace_rows(chunk):
        rows = slice(chunk * step, (chunk + 1) * step)
        x = rf_ref[0, rows, :].astype(jnp.float32)
        y = tap_weights[0] * pltpu.roll(x, 1, 1)
        y = y + tap_weights[1] * x
        y = y + tap_weights[2] * pltpu.roll(x, samples - 1, 1)
        y = y + tap_weights[3] * pltpu.roll(x, samples - 2, 1)
        y = y.astype(jnp.bfloat16).astype(jnp.float32)
        move = relative[rows, :]
        fine = move & (LANES - 1)
        reach = lane_iota((step, LANES)) + fine
        spot = reach & (LANES - 1)
        parts = [
            jnp.take_along_axis(y[:, j * LANES : (j + 1) * LANES], spot, axis=1)
            for j in range(blocks)
        ]
        stay = reach < LANES
        parts = [jnp.where(stay, parts[j], parts[(j + 1) % blocks]) for j in range(blocks)]
        for bit in range(3):
            here = (move & (LANES << bit)) != 0
            parts = [
                jnp.where(here, parts[(j + (1 << bit)) % blocks], parts[j]) for j in range(blocks)
            ]
        for j in range(blocks):
            lanes = slice(j * LANES, (j + 1) * LANES)
            wide[SUB + chunk * step : SUB + (chunk + 1) * step, lanes] = parts[j]
            part = parts[j].astype(jnp.bfloat16)
            shifted[0, rows, lanes] = part
            traces_ref[rows, lanes] = part

    def shift_rows(which, chunk):
        begin = SUB + DELTAS[which] + chunk * step
        shifted[which, chunk * step : (chunk + 1) * step, :] = wide[begin : begin + step, :].astype(jnp.bfloat16)

    trace_rows(0)
    tx_copy.wait()

    sums = tx_ref[0] + base.astype(jnp.int32)
    spots_ref[...] = sums
    tall, fine_bins = 16, 64
    coarse_bins = samples // fine_bins
    packed_rows = row_iota((fine_bins, voxels)).astype(jnp.float32).astype(jnp.bfloat16)
    one, zero = jnp.ones((), jnp.bfloat16), jnp.zeros((), jnp.bfloat16)
    coarse_spots = (sums // fine_bins).astype(jnp.float32)
    fine_spots = (sums & (fine_bins - 1)).astype(jnp.float32)

    def one_hot(spots, r, bins):
        line = jnp.broadcast_to(spots[r : r + 1, :], (tall, voxels)).astype(jnp.bfloat16)
        line = jnp.concatenate([line] * (bins // tall), axis=0)
        return jnp.where(line == packed_rows[0:bins], one, zero)

    def count_region(r):
        at = (r // 4 % 2 * (regions // 2) + r // 8 * 4 + r % 4) * coarse_bins
        count32[at : at + coarse_bins, :] = lax.dot_general(
            one_hot(coarse_spots, r, coarse_bins),
            one_hot(fine_spots, r, fine_bins),
            (((1,), (1,)), ((), ())),
            preferred_element_type=jnp.float32,
        )

    chunks = WIDTH // step
    for chunk in range(chunks):
        if chunk:
            trace_rows(chunk)
        for r in range(chunk * regions // chunks, (chunk + 1) * regions // chunks):
            count_region(r)
    for j in range(blocks):
        both = [count32[pl.ds(2 * j + q, regions, stride=coarse_bins), :] for q in range(2)]
        count16[j * LANES : (j + 1) * LANES, :] = jnp.transpose(
            jnp.concatenate(both, axis=1)
        ).astype(jnp.bfloat16)

    element = row_iota((WIDTH, regions))
    row = element // PROBE
    column = element & (PROBE - 1)
    place = lane_iota((8, regions))
    place = place % (regions // 2) // 4 * 8 + place // (regions // 2) * 4 + place % 4
    bounds = jnp.concatenate([aperture_ref[...], jnp.zeros((4, regions), jnp.int32)], axis=0)
    bounds = jnp.take_along_axis(bounds, place, axis=1)
    row_lo, row_hi = bounds[0:1, :] - first_row, bounds[1:2, :] - first_row
    col_lo, col_hi = bounds[2:3, :], bounds[3:4, :]
    column_inside = (column >= col_lo) & (column < col_hi)
    for which, delta in enumerate(DELTAS):
        other = column + delta
        inside = column_inside & (other >= col_lo) & (other < col_hi)
        colmask[which] = inside.astype(jnp.float32).astype(jnp.bfloat16)
    row_inside = (row >= row_lo) & (row < row_hi)
    for da in range(SUB):
        other = (row + da) & (SUB - 1)
        inside = row_inside & (other >= row_lo) & (other < row_hi)
        rowmask[da] = inside.astype(jnp.float32).astype(jnp.bfloat16)

    for slot, window in enumerate(WINDOWS):
        windows[slot] = window_matrix(*window)

    def gram_terms(which):
        delta = DELTAS[which]
        reach = SUB if delta else SUB // 2 + 1
        if which:
            for chunk in range(chunks):
                shift_rows(which, chunk)
        pairs = []
        for da in range(reach):
            cut = WIDTH - da * PROBE
            pairs.append(shifted[0, 0:cut, :] * shifted[which, WIDTH - cut : WIDTH, :])
            if da:
                pairs.append(shifted[0, cut:WIDTH, :] * shifted[which, 0 : WIDTH - cut, :])
        gram = jnp.dot(
            jnp.concatenate(pairs, axis=0), count16[...], preferred_element_type=jnp.float32
        ).astype(jnp.bfloat16)
        for da in range(reach):
            grams[which, da] = gram[da * WIDTH : (da + 1) * WIDTH] * colmask[which] * rowmask[da]

    def put(tile, terms):
        left = jnp.concatenate([windows[WINDOWS.index((delta, half, turn))] for delta, half, turn, da in terms], axis=1)
        right = jnp.concatenate([grams[DELTAS.index(delta), da] for delta, half, turn, da in terms], axis=0)
        out = jnp.dot(left, right, preferred_element_type=jnp.float32)
        out = jnp.transpose(out).astype(jnp.bfloat16)
        top, bottom = out[: regions // 2], out[regions // 2 :]
        at = (tile // (TILES // 2), slice(None), pl.ds(tile % (TILES // 2) * LANES, LANES))
        keep_ref[at] = jnp.where(core == 0, top, bottom)
        send_ref[at] = jnp.where(core == 0, bottom, top)

    for delta in (1, -7, 2, -6):
        gram_terms(DELTAS.index(delta))
    gram_terms(DELTAS.index(3))
    for da in range(SUB):
        put(da, ((1, 0, 0, da), (-7, 0, 0, da), (2, 1, 0, da), (-6, 1, 0, da)))
    gram_terms(DELTAS.index(-5))
    gram_terms(DELTAS.index(4))
    for da in range(SUB // 2):
        put(SUB + da, ((3, 0, 0, da), (-5, 0, 0, da), (3, 1, 0, da + 4), (-5, 1, 0, da + 4)))
    gram_terms(DELTAS.index(0))
    for da in range(SUB // 2):
        put(12 + da, ((4, 0, 0, da), (4, 0, da + 4, da + 4), (0, 1, 0, da)))
    put(16, ((0, 0, 0, 4),))
    last = (TILES // 2 - 1) * LANES
    for ref in (keep_ref, send_ref):
        ref[1, :, last:] = jnp.zeros((regions // 2, LANES), ref.dtype)


def stats(elem, reg, rf, tx_delay, rx_delay, aperture):
    regions = rx_delay.shape[0]
    samples = rf.shape[-1]
    voxels = tx_delay.shape[-1]
    vmem = pl.BlockSpec(memory_space=pltpu.VMEM)
    smem = pl.BlockSpec(memory_space=pltpu.SMEM)
    share = jax.ShapeDtypeStruct((2, regions // 2, TILES // 2 * LANES), jnp.bfloat16)
    return pl.pallas_call(
        stats_kernel,
        in_specs=[smem, smem, vmem, pl.BlockSpec(memory_space=pltpu.HBM), vmem, vmem],
        out_specs=[vmem] * 4,
        out_shape=[
            share,
            share,
            jax.ShapeDtypeStruct((WIDTH, samples), jnp.bfloat16),
            jax.ShapeDtypeStruct((regions, voxels), jnp.int32),
        ],
        scratch_shapes=[
            pltpu.VMEM((1, regions, voxels), tx_delay.dtype),
            pltpu.SemaphoreType.DMA,
            pltpu.VMEM((WIDTH + 2 * SUB, samples), jnp.float32),
            pltpu.VMEM((len(DELTAS), WIDTH, samples), jnp.bfloat16),
            pltpu.VMEM((samples // 64 * regions, 64), jnp.float32),
            pltpu.VMEM((samples, regions), jnp.bfloat16),
            pltpu.VMEM((len(DELTAS), WIDTH, regions), jnp.bfloat16),
            pltpu.VMEM((SUB, WIDTH, regions), jnp.bfloat16),
            pltpu.VMEM((len(WINDOWS), LANES, WIDTH), jnp.bfloat16),
            pltpu.VMEM((len(DELTAS), SUB, WIDTH, regions), jnp.bfloat16),
        ],
        compiler_params=pltpu.CompilerParams(vmem_limit_bytes=44 * 1024 * 1024),
        name="stats",
    )(elem, reg, rf, tx_delay, rx_delay, aperture)


def solve_kernel(total_ref, weights_ref):
    total = total_ref[...]
    per = TILES // 2
    tiles = [total[t // per : t // per + 1, t % per * LANES : (t % per + 1) * LANES] for t in range(TILES)]
    tall = jnp.concatenate(tiles + [jnp.zeros((LANES - TILES, LANES), jnp.float32)], axis=0)
    turned = jnp.transpose(tall)
    table = jnp.concatenate([turned[0:ORDER, 0:ORDER], turned[ORDER:LANES, 0:ORDER]], axis=1)
    i = row_iota((ORDER, LANES))
    lane = lane_iota((ORDER, LANES))
    j = lane & (ORDER - 1)
    da = ((j // SUB) - (i // SUB)) & (SUB - 1)
    d = ((j & (SUB - 1)) - (i & (SUB - 1))) & (SUB - 1)
    low = (i & (SUB - 1)) < 4
    spot = jnp.where(
        d == 1, da,
        jnp.where(
            d == 2, da + ORDER,
            jnp.where(
                d == 3, SUB + (da & 3) + ORDER * (da // 4),
                jnp.where(d == 4, jnp.where(low, 12 + da, 16 - da), jnp.where(da == 4, 16, 12 + da + ORDER)),
            ),
        ),
    )
    stored = ((d >= 1) & (d <= 3)) | ((d == 0) & (da <= 4))
    stored |= (d == 4) & ((low & (da <= 3)) | (~low & (da >= 1) & (da <= 4)))
    half = jnp.take_along_axis(table, spot & (LANES - 1), axis=1)
    half = jnp.where(stored & (lane < ORDER), half, 0.0)
    square = jnp.concatenate([half, jnp.zeros((LANES - ORDER, LANES), jnp.float32)], axis=0)
    cov = jnp.where(stored, half, jnp.transpose(square)[0:ORDER, :])
    diagonal = lane == i
    trace = jnp.sum(jnp.sum(jnp.where(diagonal, cov, 0.0), axis=1, keepdims=True), axis=0, keepdims=True)
    cov = cov + jnp.where(diagonal, load_factor * trace / ORDER, 0.0)
    work = jnp.where(lane < ORDER, cov, 1.0)
    high = 8
    shape = (high, LANES)
    sublane = row_iota(shape)
    groups = [work[g : g + high, :] for g in range(0, ORDER, high)]
    def spread(part, k):
        return jnp.broadcast_to(part[:, k : k + 1], shape)

    for k in range(0, ORDER, 4):
        at, inner = k // high, k % high
        rows = [jnp.broadcast_to(groups[at][inner + n : inner + n + 1, :], shape) for n in range(4)]
        m = [[spread(rows[n], k + c) for c in range(4)] for n in range(4)]
        inverse = 1.0 / (m[0][0] * m[1][1] - m[0][1] * m[1][0])
        i00, i01 = m[1][1] * inverse, -m[0][1] * inverse
        i10, i11 = -m[1][0] * inverse, m[0][0] * inverse
        e02, e03 = i00 * m[0][2] + i01 * m[1][2], i00 * m[0][3] + i01 * m[1][3]
        e12, e13 = i10 * m[0][2] + i11 * m[1][2], i10 * m[0][3] + i11 * m[1][3]
        first = i00 * rows[0] + i01 * rows[1]
        second = i10 * rows[0] + i11 * rows[1]
        third = rows[2] - m[2][0] * first - m[2][1] * second
        fourth = rows[3] - m[3][0] * first - m[3][1] * second
        s22 = m[2][2] - m[2][0] * e02 - m[2][1] * e12
        s23 = m[2][3] - m[2][0] * e03 - m[2][1] * e13
        s32 = m[3][2] - m[3][0] * e02 - m[3][1] * e12
        s33 = m[3][3] - m[3][0] * e03 - m[3][1] * e13
        inverse = 1.0 / (s22 * s33 - s23 * s32)
        third, fourth = (third * s33 - fourth * s23) * inverse, (fourth * s22 - third * s32) * inverse
        first = first - e02 * third - e03 * fourth
        second = second - e12 * third - e13 * fourth
        solved_rows = (first, second, third, fourth)
        updated = []
        for g, part in enumerate(groups):
            change = sum(spread(part, k + c) * solved_rows[c] for c in range(4))
            new = part - change
            if g == at:
                for c in range(4):
                    new = jnp.where(sublane == inner + c, solved_rows[c], new)
            updated.append(new)
        groups = updated
    solved = jnp.concatenate(groups, axis=0)[:, ORDER : ORDER + 1]
    row = jnp.sum(jnp.where(diagonal, solved, 0.0), axis=0, keepdims=True)
    weights_ref[...] = row / jnp.sum(row, axis=1, keepdims=True)


def solve(parts):
    return pl.pallas_call(
        solve_kernel,
        out_shape=jax.ShapeDtypeStruct((1, LANES), jnp.float32),
        compiler_params=pltpu.CompilerParams(vmem_limit_bytes=32 * 1024 * 1024),
        name="solve",
    )(parts)


def image_kernel(scale, elem, weights_ref, traces_ref, spots_ref, aperture_ref, out_ref, line_ref):
    regions, voxels = spots_ref.shape
    samples = traces_ref.shape[-1]
    first_row = elem[0] * SUB

    source = row_iota((LANES, WIDTH))
    element = lane_iota((LANES, WIDTH))
    x = source & (SUB - 1)
    k = element & (PROBE - 1)
    spread = (source // SUB == element // PROBE) & (k >= x) & (k <= x + PROBE - SUB)
    spread = spread.astype(jnp.float32).astype(jnp.bfloat16)
    weights = weights_ref[...]
    high, low = split(weights)
    gain = jnp.dot(high, spread, preferred_element_type=jnp.float32)
    gain = gain + jnp.dot(low, spread, preferred_element_type=jnp.float32)
    lane = lane_iota((regions, WIDTH))
    row = lane // PROBE + first_row
    column = lane & (PROBE - 1)
    bounds = aperture_ref[...].astype(jnp.float32)
    bounds = jnp.concatenate([bounds, jnp.zeros((LANES - 4, regions), jnp.float32)], axis=0)
    bounds = jnp.transpose(bounds).astype(jnp.int32)
    inside = (row >= bounds[:, 0:1]) & (row < bounds[:, 1:2])
    inside &= (column >= bounds[:, 2:3]) & (column < bounds[:, 3:4])
    high, low = split(jnp.where(inside, gain * scale, 0.0))
    both = jnp.dot(
        jnp.concatenate([high, low], axis=0), traces_ref[...], preferred_element_type=jnp.float32
    )
    line_ref[...] = both[:regions] + both[regions:]

    sums = spots_ref[...]
    own = out_ref.shape[2]
    group = 32
    blocks = samples // LANES
    near = 9
    for begin in range(0, regions, group):
        rows = slice(begin, begin + group)
        spots = sums[rows, :]
        first = jnp.minimum(jnp.min(spots, axis=1, keepdims=True) // LANES, blocks - near)
        first = jnp.broadcast_to(first, (group, LANES))
        parts = [line_ref[rows, j * LANES : (j + 1) * LANES] for j in range(blocks)]
        for bit in (4, 2, 1):
            here = (first & bit) != 0
            parts = [jnp.where(here, parts[j + bit], parts[j]) for j in range(near - 1 + bit)]
        for v in range(voxels // LANES):
            spot = spots[:, v * LANES : (v + 1) * LANES]
            fine = spot & (LANES - 1)
            coarse = spot // LANES - first
            picked = jnp.zeros((group, LANES), jnp.float32)
            for j in range(near):
                found = jnp.take_along_axis(parts[j], fine, axis=1)
                picked = jnp.where(coarse == j, found, picked)
            out_ref[begin // own : (begin + group) // own, v] = picked.reshape(group // own, own, LANES)


def image(scale, n_reg, elem, weights, traces, spots, aperture):
    regions, voxels = spots.shape
    samples = traces.shape[-1]
    vmem = pl.BlockSpec(memory_space=pltpu.VMEM)
    return pl.pallas_call(
        functools.partial(image_kernel, scale),
        in_specs=[pl.BlockSpec(memory_space=pltpu.SMEM), vmem, vmem, vmem, vmem],
        out_specs=vmem,
        out_shape=jax.ShapeDtypeStruct((n_reg, voxels // LANES, regions // n_reg, LANES), jnp.float32),
        scratch_shapes=[pltpu.VMEM((regions, samples), jnp.float32)],
        compiler_params=pltpu.CompilerParams(vmem_limit_bytes=32 * 1024 * 1024),
        name="image",
    )(elem, weights, traces, spots, aperture)


REG = ("xy", "core")
BOTH = ("xy", "core", "elem")
CHIPS = ("xy", "elem")


def per_device(rf, tx_delay, rx_delay, aperture):
    n_reg = lax.axis_size("xy") * lax.axis_size("core")
    n_elem = lax.axis_size("elem")
    regions, voxels = rx_delay.shape[0], tx_delay.shape[2]
    devices = n_reg * n_elem
    scale = 8.0 / math.sqrt(n_reg * n_elem * SHIFTS)
    elem = lax.axis_index("elem").astype(jnp.int32).reshape(1)
    reg = lax.axis_index(REG).astype(jnp.int32).reshape(1)
    bounds = aperture.T
    keep, send, traces, spots = stats(elem, reg, rf, tx_delay, rx_delay, bounds)
    other = lax.ppermute(send, "core", [(0, 1), (1, 0)])
    chip = (keep.astype(jnp.float32) + other.astype(jnp.float32)).astype(jnp.bfloat16)
    parts = lax.all_to_all(chip.transpose(1, 0, 2), CHIPS, 0, 0, tiled=True)
    mine = solve(jnp.sum(parts.astype(jnp.float32), axis=0))
    weights = lax.all_to_all(jnp.broadcast_to(mine, (devices, LANES)), BOTH, 0, 0, tiled=True)
    partial = image(scale, n_reg, elem, weights, traces, spots, bounds)
    owned = partial.reshape(devices, regions // n_reg, voxels // n_elem)
    arrived = lax.all_to_all(owned, BOTH, 0, 0, tiled=True)
    return jnp.sum(arrived, axis=0)


def solution(mesh):
    n_elem, n_reg = mesh.shape["elem"], mesh.shape["reg"]
    chips = jax.sharding.Mesh(mesh.devices.reshape(n_elem, n_reg // 2, 2), ("elem", "xy", "core"))
    in_specs = (P(REG, "elem", None), P(), P(None, "elem"), P())
    out_specs = P(REG, "elem")
    return jax.shard_map(
        per_device, mesh=chips, in_specs=in_specs, out_specs=out_specs, check_vma=False
    )
```

```python
import functools
import math

import jax
import jax.numpy as jnp
from jax import lax
from jax.experimental import pallas as pl
from jax.experimental.pallas import tpu as pltpu
from jax.sharding import PartitionSpec as P

PROBE = 32
SUB = 8
SHIFTS = PROBE - SUB + 1
WIDTH = SUB * PROBE
ORDER = SUB * SUB
LANES = 128

tap_weights = (-0.0625, 0.5625, 0.5625, -0.0625)
load_factor = 0.05

DELTAS = (0, 1, 2, 3, 4, -5, -6, -7)
TILES = 18
WINDOWS = (
    (1, 0, 0), (-7, 0, 0), (2, 1, 0), (-6, 1, 0), (3, 0, 0), (-5, 0, 0), (3, 1, 0), (-5, 1, 0),
    (4, 0, 0), (4, 0, 4), (4, 0, 5), (4, 0, 6), (4, 0, 7), (0, 1, 0), (0, 0, 0),
)


def lane_iota(shape):
    return lax.broadcasted_iota(jnp.int32, shape, len(shape) - 1)


def row_iota(shape):
    return lax.broadcasted_iota(jnp.int32, shape, 0)


def window_matrix(delta, half, turn):
    element = lane_iota((LANES, WIDTH))
    target = row_iota((LANES, WIDTH)) - ORDER * half
    x = target & (SUB - 1)
    k = element & (PROBE - 1)
    good = (target >= 0) & (target < ORDER)
    if turn:
        x = x - 4
        good &= x >= 0
    good &= ((element // PROBE + turn) & (SUB - 1)) == (target // SUB)
    good &= (k >= x) & (k <= x + PROBE - SUB)
    good &= (x + delta >= 0) & (x + delta < SUB)
    return good.astype(jnp.float32).astype(jnp.bfloat16)


def split(x):
    high = x.astype(jnp.bfloat16)
    low = (x - high.astype(jnp.float32)).astype(jnp.bfloat16)
    return high, low


def stats_kernel(elem, reg, rf_ref, tx_hbm, rx_ref, aperture_ref, keep_ref, send_ref, traces_ref, spots_ref,
                 tx_ref, arrival,
                 wide, shifted, count32, count16, colmask, rowmask, windows, grams):
    tx_copy = pltpu.make_async_copy(tx_hbm.at[pl.ds(reg[0], 1)], tx_ref, arrival)
    tx_copy.start()
    core = reg[0] & 1
    regions = rx_ref.shape[0]
    samples = rf_ref.shape[-1]
    blocks = samples // LANES
    voxels = tx_ref.shape[-1]
    first_row = elem[0] * SUB

    rx = rx_ref[...].astype(jnp.float32)
    base = jnp.min(rx, axis=1, keepdims=True)
    lead = rx[0:1, :] - base[0:1, :]
    relative = jnp.transpose(jnp.broadcast_to(lead, (LANES, WIDTH))).astype(jnp.int32)
    wide[0:SUB, :] = jnp.zeros((SUB, samples), jnp.float32)
    wide[SUB + WIDTH : 2 * SUB + WIDTH, :] = jnp.zeros((SUB, samples), jnp.float32)
    step = 32

    def trace_rows(chunk):
        rows = slice(chunk * step, (chunk + 1) * step)
        x = rf_ref[0, rows, :].astype(jnp.float32)
        y = tap_weights[0] * pltpu.roll(x, 1, 1)
        y = y + tap_weights[1] * x
        y = y + tap_weights[2] * pltpu.roll(x, samples - 1, 1)
        y = y + tap_weights[3] * pltpu.roll(x, samples - 2, 1)
        y = y.astype(jnp.bfloat16).astype(jnp.float32)
        move = relative[rows, :]
        fine = move & (LANES - 1)
        reach = lane_iota((step, LANES)) + fine
        spot = reach & (LANES - 1)
        parts = [
            jnp.take_along_axis(y[:, j * LANES : (j + 1) * LANES], spot, axis=1)
            for j in range(blocks)
        ]
        stay = reach < LANES
        parts = [jnp.where(stay, parts[j], parts[(j + 1) % blocks]) for j in range(blocks)]
        for bit in range(3):
            here = (move & (LANES << bit)) != 0
            parts = [
                jnp.where(here, parts[(j + (1 << bit)) % blocks], parts[j]) for j in range(blocks)
            ]
        for j in range(blocks):
            lanes = slice(j * LANES, (j + 1) * LANES)
            wide[SUB + chunk * step : SUB + (chunk + 1) * step, lanes] = parts[j]
            part = parts[j].astype(jnp.bfloat16)
            shifted[0, rows, lanes] = part
            traces_ref[rows, lanes] = part

    def shift_rows(which, chunk):
        begin = SUB + DELTAS[which] + chunk * step
        shifted[which, chunk * step : (chunk + 1) * step, :] = wide[begin : begin + step, :].astype(jnp.bfloat16)

    trace_rows(0)
    tx_copy.wait()

    sums = tx_ref[0] + base.astype(jnp.int32)
    spots_ref[...] = sums
    tall, fine_bins = 16, 64
    coarse_bins = samples // fine_bins
    packed_rows = row_iota((fine_bins, voxels)).astype(jnp.float32).astype(jnp.bfloat16)
    one, zero = jnp.ones((), jnp.bfloat16), jnp.zeros((), jnp.bfloat16)
    coarse_spots = (sums // fine_bins).astype(jnp.float32)
    fine_spots = (sums & (fine_bins - 1)).astype(jnp.float32)

    def one_hot(spots, r, bins):
        line = jnp.broadcast_to(spots[r : r + 1, :], (tall, voxels)).astype(jnp.bfloat16)
        line = jnp.concatenate([line] * (bins // tall), axis=0)
        return jnp.where(line == packed_rows[0:bins], one, zero)

    def count_region(r):
        at = (r // 4 % 2 * (regions // 2) + r // 8 * 4 + r % 4) * coarse_bins
        count32[at : at + coarse_bins, :] = lax.dot_general(
            one_hot(coarse_spots, r, coarse_bins),
            one_hot(fine_spots, r, fine_bins),
            (((1,), (1,)), ((), ())),
            preferred_element_type=jnp.float32,
        )

    chunks = WIDTH // step
    for chunk in range(chunks):
        if chunk:
            trace_rows(chunk)
        for r in range(chunk * regions // chunks, (chunk + 1) * regions // chunks):
            count_region(r)
    for j in range(blocks):
        both = [count32[pl.ds(2 * j + q, regions, stride=coarse_bins), :] for q in range(2)]
        count16[j * LANES : (j + 1) * LANES, :] = jnp.transpose(
            jnp.concatenate(both, axis=1)
        ).astype(jnp.bfloat16)

    element = row_iota((WIDTH, regions))
    row = element // PROBE
    column = element & (PROBE - 1)
    place = lane_iota((8, regions))
    place = place % (regions // 2) // 4 * 8 + place // (regions // 2) * 4 + place % 4
    bounds = jnp.concatenate([aperture_ref[...], jnp.zeros((4, regions), jnp.int32)], axis=0)
    bounds = jnp.take_along_axis(bounds, place, axis=1)
    row_lo, row_hi = bounds[0:1, :] - first_row, bounds[1:2, :] - first_row
    col_lo, col_hi = bounds[2:3, :], bounds[3:4, :]
    column_inside = (column >= col_lo) & (column < col_hi)
    for which, delta in enumerate(DELTAS):
        other = column + delta
        inside = column_inside & (other >= col_lo) & (other < col_hi)
        colmask[which] = inside.astype(jnp.float32).astype(jnp.bfloat16)
    row_inside = (row >= row_lo) & (row < row_hi)
    for da in range(SUB):
        other = (row + da) & (SUB - 1)
        inside = row_inside & (other >= row_lo) & (other < row_hi)
        rowmask[da] = inside.astype(jnp.float32).astype(jnp.bfloat16)

    for slot, window in enumerate(WINDOWS):
        windows[slot] = window_matrix(*window)

    def gram_terms(which):
        delta = DELTAS[which]
        reach = SUB if delta else SUB // 2 + 1
        if which:
            for chunk in range(chunks):
                shift_rows(which, chunk)
        group = 4
        for begin in range(0, reach, group):
            held = range(begin, min(begin + group, reach))
            pairs = []
            for da in held:
                cut = WIDTH - da * PROBE
                pairs.append(shifted[0, 0:cut, :] * shifted[which, WIDTH - cut : WIDTH, :])
                if da:
                    pairs.append(shifted[0, cut:WIDTH, :] * shifted[which, 0 : WIDTH - cut, :])
            gram = jnp.dot(
                jnp.concatenate(pairs, axis=0), count16[...], preferred_element_type=jnp.float32
            ).astype(jnp.bfloat16)
            for n, da in enumerate(held):
                grams[which, da] = gram[n * WIDTH : (n + 1) * WIDTH] * colmask[which] * rowmask[da]

    def put(tile, terms):
        left = jnp.concatenate([windows[WINDOWS.index((delta, half, turn))] for delta, half, turn, da in terms], axis=1)
        right = jnp.concatenate([grams[DELTAS.index(delta), da] for delta, half, turn, da in terms], axis=0)
        out = jnp.dot(left, right, preferred_element_type=jnp.float32)
        out = jnp.transpose(out).astype(jnp.bfloat16)
        top, bottom = out[: regions // 2], out[regions // 2 :]
        at = (tile // (TILES // 2), slice(None), pl.ds(tile % (TILES // 2) * LANES, LANES))
        keep_ref[at] = jnp.where(core == 0, top, bottom)
        send_ref[at] = jnp.where(core == 0, bottom, top)

    for delta in (1, -7, 2, -6):
        gram_terms(DELTAS.index(delta))
    gram_terms(DELTAS.index(3))
    for da in range(SUB):
        put(da, ((1, 0, 0, da), (-7, 0, 0, da), (2, 1, 0, da), (-6, 1, 0, da)))
    gram_terms(DELTAS.index(-5))
    gram_terms(DELTAS.index(4))
    for da in range(SUB // 2):
        put(SUB + da, ((3, 0, 0, da), (-5, 0, 0, da), (3, 1, 0, da + 4), (-5, 1, 0, da + 4)))
    gram_terms(DELTAS.index(0))
    for da in range(SUB // 2):
        put(12 + da, ((4, 0, 0, da), (4, 0, da + 4, da + 4), (0, 1, 0, da)))
    put(16, ((0, 0, 0, 4),))
    last = (TILES // 2 - 1) * LANES
    for ref in (keep_ref, send_ref):
        ref[1, :, last:] = jnp.zeros((regions // 2, LANES), ref.dtype)


def stats(elem, reg, rf, tx_delay, rx_delay, aperture):
    regions = rx_delay.shape[0]
    samples = rf.shape[-1]
    voxels = tx_delay.shape[-1]
    vmem = pl.BlockSpec(memory_space=pltpu.VMEM)
    smem = pl.BlockSpec(memory_space=pltpu.SMEM)
    share = jax.ShapeDtypeStruct((2, regions // 2, TILES // 2 * LANES), jnp.bfloat16)
    return pl.pallas_call(
        stats_kernel,
        in_specs=[smem, smem, vmem, pl.BlockSpec(memory_space=pltpu.HBM), vmem, vmem],
        out_specs=[vmem] * 4,
        out_shape=[
            share,
            share,
            jax.ShapeDtypeStruct((WIDTH, samples), jnp.bfloat16),
            jax.ShapeDtypeStruct((regions, voxels), jnp.int32),
        ],
        scratch_shapes=[
            pltpu.VMEM((1, regions, voxels), tx_delay.dtype),
            pltpu.SemaphoreType.DMA,
            pltpu.VMEM((WIDTH + 2 * SUB, samples), jnp.float32),
            pltpu.VMEM((len(DELTAS), WIDTH, samples), jnp.bfloat16),
            pltpu.VMEM((samples // 64 * regions, 64), jnp.float32),
            pltpu.VMEM((samples, regions), jnp.bfloat16),
            pltpu.VMEM((len(DELTAS), WIDTH, regions), jnp.bfloat16),
            pltpu.VMEM((SUB, WIDTH, regions), jnp.bfloat16),
            pltpu.VMEM((len(WINDOWS), LANES, WIDTH), jnp.bfloat16),
            pltpu.VMEM((len(DELTAS), SUB, WIDTH, regions), jnp.bfloat16),
        ],
        compiler_params=pltpu.CompilerParams(vmem_limit_bytes=44 * 1024 * 1024),
        name="stats",
    )(elem, reg, rf, tx_delay, rx_delay, aperture)


def solve_kernel(total_ref, weights_ref):
    total = total_ref[...]
    per = TILES // 2
    tiles = [total[t // per : t // per + 1, t % per * LANES : (t % per + 1) * LANES] for t in range(TILES)]
    tall = jnp.concatenate(tiles + [jnp.zeros((LANES - TILES, LANES), jnp.float32)], axis=0)
    turned = jnp.transpose(tall)
    table = jnp.concatenate([turned[0:ORDER, 0:ORDER], turned[ORDER:LANES, 0:ORDER]], axis=1)
    i = row_iota((ORDER, LANES))
    lane = lane_iota((ORDER, LANES))
    j = lane & (ORDER - 1)
    da = ((j // SUB) - (i // SUB)) & (SUB - 1)
    d = ((j & (SUB - 1)) - (i & (SUB - 1))) & (SUB - 1)
    low = (i & (SUB - 1)) < 4
    spot = jnp.where(
        d == 1, da,
        jnp.where(
            d == 2, da + ORDER,
            jnp.where(
                d == 3, SUB + (da & 3) + ORDER * (da // 4),
                jnp.where(d == 4, jnp.where(low, 12 + da, 16 - da), jnp.where(da == 4, 16, 12 + da + ORDER)),
            ),
        ),
    )
    stored = ((d >= 1) & (d <= 3)) | ((d == 0) & (da <= 4))
    stored |= (d == 4) & ((low & (da <= 3)) | (~low & (da >= 1) & (da <= 4)))
    half = jnp.take_along_axis(table, spot & (LANES - 1), axis=1)
    half = jnp.where(stored & (lane < ORDER), half, 0.0)
    square = jnp.concatenate([half, jnp.zeros((LANES - ORDER, LANES), jnp.float32)], axis=0)
    cov = jnp.where(stored, half, jnp.transpose(square)[0:ORDER, :])
    diagonal = lane == i
    trace = jnp.sum(jnp.sum(jnp.where(diagonal, cov, 0.0), axis=1, keepdims=True), axis=0, keepdims=True)
    cov = cov + jnp.where(diagonal, load_factor * trace / ORDER, 0.0)
    work = jnp.where(lane < ORDER, cov, 1.0)
    high = 8
    shape = (high, LANES)
    sublane = row_iota(shape)
    groups = [work[g : g + high, :] for g in range(0, ORDER, high)]
    def spread(part, k):
        return jnp.broadcast_to(part[:, k : k + 1], shape)

    for k in range(0, ORDER, 4):
        at, inner = k // high, k % high
        rows = [jnp.broadcast_to(groups[at][inner + n : inner + n + 1, :], shape) for n in range(4)]
        m = [[spread(rows[n], k + c) for c in range(4)] for n in range(4)]
        inverse = 1.0 / (m[0][0] * m[1][1] - m[0][1] * m[1][0])
        i00, i01 = m[1][1] * inverse, -m[0][1] * inverse
        i10, i11 = -m[1][0] * inverse, m[0][0] * inverse
        e02, e03 = i00 * m[0][2] + i01 * m[1][2], i00 * m[0][3] + i01 * m[1][3]
        e12, e13 = i10 * m[0][2] + i11 * m[1][2], i10 * m[0][3] + i11 * m[1][3]
        first = i00 * rows[0] + i01 * rows[1]
        second = i10 * rows[0] + i11 * rows[1]
        third = rows[2] - m[2][0] * first - m[2][1] * second
        fourth = rows[3] - m[3][0] * first - m[3][1] * second
        s22 = m[2][2] - m[2][0] * e02 - m[2][1] * e12
        s23 = m[2][3] - m[2][0] * e03 - m[2][1] * e13
        s32 = m[3][2] - m[3][0] * e02 - m[3][1] * e12
        s33 = m[3][3] - m[3][0] * e03 - m[3][1] * e13
        inverse = 1.0 / (s22 * s33 - s23 * s32)
        third, fourth = (third * s33 - fourth * s23) * inverse, (fourth * s22 - third * s32) * inverse
        first = first - e02 * third - e03 * fourth
        second = second - e12 * third - e13 * fourth
        solved_rows = (first, second, third, fourth)
        updated = []
        for g, part in enumerate(groups):
            change = sum(spread(part, k + c) * solved_rows[c] for c in range(4))
            new = part - change
            if g == at:
                for c in range(4):
                    new = jnp.where(sublane == inner + c, solved_rows[c], new)
            updated.append(new)
        groups = updated
    solved = jnp.concatenate(groups, axis=0)[:, ORDER : ORDER + 1]
    row = jnp.sum(jnp.where(diagonal, solved, 0.0), axis=0, keepdims=True)
    weights_ref[...] = row / jnp.sum(row, axis=1, keepdims=True)


def solve(parts):
    return pl.pallas_call(
        solve_kernel,
        out_shape=jax.ShapeDtypeStruct((1, LANES), jnp.float32),
        compiler_params=pltpu.CompilerParams(vmem_limit_bytes=32 * 1024 * 1024),
        name="solve",
    )(parts)


def image_kernel(scale, elem, weights_ref, traces_ref, spots_ref, aperture_ref, out_ref, line_ref):
    regions, voxels = spots_ref.shape
    samples = traces_ref.shape[-1]
    first_row = elem[0] * SUB

    source = row_iota((LANES, WIDTH))
    element = lane_iota((LANES, WIDTH))
    x = source & (SUB - 1)
    k = element & (PROBE - 1)
    spread = (source // SUB == element // PROBE) & (k >= x) & (k <= x + PROBE - SUB)
    spread = spread.astype(jnp.float32).astype(jnp.bfloat16)
    weights = weights_ref[...]
    high, low = split(weights)
    gain = jnp.dot(high, spread, preferred_element_type=jnp.float32)
    gain = gain + jnp.dot(low, spread, preferred_element_type=jnp.float32)
    lane = lane_iota((regions, WIDTH))
    row = lane // PROBE + first_row
    column = lane & (PROBE - 1)
    bounds = aperture_ref[...].astype(jnp.float32)
    bounds = jnp.concatenate([bounds, jnp.zeros((LANES - 4, regions), jnp.float32)], axis=0)
    bounds = jnp.transpose(bounds).astype(jnp.int32)
    inside = (row >= bounds[:, 0:1]) & (row < bounds[:, 1:2])
    inside &= (column >= bounds[:, 2:3]) & (column < bounds[:, 3:4])
    high, low = split(jnp.where(inside, gain * scale, 0.0))
    both = jnp.dot(
        jnp.concatenate([high, low], axis=0), traces_ref[...], preferred_element_type=jnp.float32
    )
    line_ref[...] = both[:regions] + both[regions:]

    sums = spots_ref[...]
    own = out_ref.shape[2]
    group = 32
    blocks = samples // LANES
    near = 9
    for begin in range(0, regions, group):
        rows = slice(begin, begin + group)
        spots = sums[rows, :]
        first = jnp.minimum(jnp.min(spots, axis=1, keepdims=True) // LANES, blocks - near)
        first = jnp.broadcast_to(first, (group, LANES))
        parts = [line_ref[rows, j * LANES : (j + 1) * LANES] for j in range(blocks)]
        for bit in (4, 2, 1):
            here = (first & bit) != 0
            parts = [jnp.where(here, parts[j + bit], parts[j]) for j in range(near - 1 + bit)]
        for v in range(voxels // LANES):
            spot = spots[:, v * LANES : (v + 1) * LANES]
            fine = spot & (LANES - 1)
            coarse = spot // LANES - first
            picked = jnp.zeros((group, LANES), jnp.float32)
            for j in range(near):
                found = jnp.take_along_axis(parts[j], fine, axis=1)
                picked = jnp.where(coarse == j, found, picked)
            out_ref[begin // own : (begin + group) // own, v] = picked.reshape(group // own, own, LANES)


def image(scale, n_reg, elem, weights, traces, spots, aperture):
    regions, voxels = spots.shape
    samples = traces.shape[-1]
    vmem = pl.BlockSpec(memory_space=pltpu.VMEM)
    return pl.pallas_call(
        functools.partial(image_kernel, scale),
        in_specs=[pl.BlockSpec(memory_space=pltpu.SMEM), vmem, vmem, vmem, vmem],
        out_specs=vmem,
        out_shape=jax.ShapeDtypeStruct((n_reg, voxels // LANES, regions // n_reg, LANES), jnp.float32),
        scratch_shapes=[pltpu.VMEM((regions, samples), jnp.float32)],
        compiler_params=pltpu.CompilerParams(vmem_limit_bytes=32 * 1024 * 1024),
        name="image",
    )(elem, weights, traces, spots, aperture)


REG = ("xy", "core")
BOTH = ("xy", "core", "elem")
CHIPS = ("xy", "elem")


def per_device(rf, tx_delay, rx_delay, aperture):
    n_reg = lax.axis_size("xy") * lax.axis_size("core")
    n_elem = lax.axis_size("elem")
    regions, voxels = rx_delay.shape[0], tx_delay.shape[2]
    devices = n_reg * n_elem
    scale = 8.0 / math.sqrt(n_reg * n_elem * SHIFTS)
    elem = lax.axis_index("elem").astype(jnp.int32).reshape(1)
    reg = lax.axis_index(REG).astype(jnp.int32).reshape(1)
    bounds = aperture.T
    keep, send, traces, spots = stats(elem, reg, rf, tx_delay, rx_delay, bounds)
    other = lax.ppermute(send, "core", [(0, 1), (1, 0)])
    chip = (keep.astype(jnp.float32) + other.astype(jnp.float32)).astype(jnp.bfloat16)
    parts = lax.all_to_all(chip.transpose(1, 0, 2), CHIPS, 0, 0, tiled=True)
    mine = solve(jnp.sum(parts.astype(jnp.float32), axis=0))
    weights = lax.all_to_all(jnp.broadcast_to(mine, (devices, LANES)), BOTH, 0, 0, tiled=True)
    partial = image(scale, n_reg, elem, weights, traces, spots, bounds)
    owned = partial.reshape(devices, regions // n_reg, voxels // n_elem)
    arrived = lax.all_to_all(owned, BOTH, 0, 0, tiled=True)
    return jnp.sum(arrived, axis=0)


def solution(mesh):
    n_elem, n_reg = mesh.shape["elem"], mesh.shape["reg"]
    chips = jax.sharding.Mesh(mesh.devices.reshape(n_elem, n_reg // 2, 2), ("elem", "xy", "core"))
    in_specs = (P(REG, "elem", None), P(), P(None, "elem"), P())
    out_specs = P(REG, "elem")
    return jax.shard_map(
        per_device, mesh=chips, in_specs=in_specs, out_specs=out_specs, check_vma=False
    )
```

```python
import functools
import math

import jax
import jax.numpy as jnp
from jax import lax
from jax.experimental import pallas as pl
from jax.experimental.pallas import tpu as pltpu
from jax.sharding import PartitionSpec as P

PROBE = 32
SUB = 8
SHIFTS = PROBE - SUB + 1
WIDTH = SUB * PROBE
ORDER = SUB * SUB
LANES = 128

tap_weights = (-0.0625, 0.5625, 0.5625, -0.0625)
load_factor = 0.05

DELTAS = (0, 1, 2, 3, 4, -5, -6, -7)
TILES = 18
WINDOWS = (
    (1, 0, 0), (-7, 0, 0), (2, 1, 0), (-6, 1, 0), (3, 0, 0), (-5, 0, 0), (3, 1, 0), (-5, 1, 0),
    (4, 0, 0), (4, 0, 4), (4, 0, 5), (4, 0, 6), (4, 0, 7), (0, 1, 0), (0, 0, 0),
)


def lane_iota(shape):
    return lax.broadcasted_iota(jnp.int32, shape, len(shape) - 1)


def row_iota(shape):
    return lax.broadcasted_iota(jnp.int32, shape, 0)


def window_matrix(delta, half, turn):
    element = lane_iota((LANES, WIDTH))
    target = row_iota((LANES, WIDTH)) - ORDER * half
    x = target & (SUB - 1)
    k = element & (PROBE - 1)
    good = (target >= 0) & (target < ORDER)
    if turn:
        x = x - 4
        good &= x >= 0
    good &= ((element // PROBE + turn) & (SUB - 1)) == (target // SUB)
    good &= (k >= x) & (k <= x + PROBE - SUB)
    good &= (x + delta >= 0) & (x + delta < SUB)
    return good.astype(jnp.float32).astype(jnp.bfloat16)


def split(x):
    high = x.astype(jnp.bfloat16)
    low = (x - high.astype(jnp.float32)).astype(jnp.bfloat16)
    return high, low


def stats_kernel(elem, reg, rf_ref, tx_hbm, rx_ref, aperture_ref, keep_ref, send_ref, traces_ref, spots_ref,
                 tx_ref, arrival,
                 wide, shifted, count32, count16, colmask, rowmask, windows, grams):
    tx_copy = pltpu.make_async_copy(tx_hbm.at[pl.ds(reg[0], 1)], tx_ref, arrival)
    tx_copy.start()
    core = reg[0] & 1
    regions = rx_ref.shape[0]
    samples = rf_ref.shape[-1]
    blocks = samples // LANES
    voxels = tx_ref.shape[-1]
    first_row = elem[0] * SUB

    rx = rx_ref[...].astype(jnp.float32)
    base = jnp.min(rx, axis=1, keepdims=True)
    lead = rx[0:1, :] - base[0:1, :]
    relative = jnp.transpose(jnp.broadcast_to(lead, (LANES, WIDTH))).astype(jnp.int32)
    wide[0:SUB, :] = jnp.zeros((SUB, samples), jnp.float32)
    wide[SUB + WIDTH : 2 * SUB + WIDTH, :] = jnp.zeros((SUB, samples), jnp.float32)
    step = 32

    def trace_rows(chunk):
        rows = slice(chunk * step, (chunk + 1) * step)
        x = rf_ref[0, rows, :].astype(jnp.float32)
        y = tap_weights[0] * pltpu.roll(x, 1, 1)
        y = y + tap_weights[1] * x
        y = y + tap_weights[2] * pltpu.roll(x, samples - 1, 1)
        y = y + tap_weights[3] * pltpu.roll(x, samples - 2, 1)
        y = y.astype(jnp.bfloat16).astype(jnp.float32)
        move = relative[rows, :]
        fine = move & (LANES - 1)
        reach = lane_iota((step, LANES)) + fine
        spot = reach & (LANES - 1)
        parts = [
            jnp.take_along_axis(y[:, j * LANES : (j + 1) * LANES], spot, axis=1)
            for j in range(blocks)
        ]
        stay = reach < LANES
        parts = [jnp.where(stay, parts[j], parts[(j + 1) % blocks]) for j in range(blocks)]
        for bit in range(3):
            here = (move & (LANES << bit)) != 0
            parts = [
                jnp.where(here, parts[(j + (1 << bit)) % blocks], parts[j]) for j in range(blocks)
            ]
        for j in range(blocks):
            lanes = slice(j * LANES, (j + 1) * LANES)
            wide[SUB + chunk * step : SUB + (chunk + 1) * step, lanes] = parts[j]
            part = parts[j].astype(jnp.bfloat16)
            shifted[0, rows, lanes] = part
            traces_ref[rows, lanes] = part

    def shift_rows(which, chunk):
        begin = SUB + DELTAS[which] + chunk * step
        shifted[which, chunk * step : (chunk + 1) * step, :] = wide[begin : begin + step, :].astype(jnp.bfloat16)

    trace_rows(0)
    tx_copy.wait()

    sums = tx_ref[0] + base.astype(jnp.int32)
    spots_ref[...] = sums
    tall, fine_bins = 16, 64
    coarse_bins = samples // fine_bins
    packed_rows = row_iota((fine_bins, voxels)).astype(jnp.float32).astype(jnp.bfloat16)
    one, zero = jnp.ones((), jnp.bfloat16), jnp.zeros((), jnp.bfloat16)
    coarse_spots = (sums // fine_bins).astype(jnp.float32)
    fine_spots = (sums & (fine_bins - 1)).astype(jnp.float32)

    def one_hot(spots, r, bins):
        line = jnp.broadcast_to(spots[r : r + 1, :], (tall, voxels)).astype(jnp.bfloat16)
        line = jnp.concatenate([line] * (bins // tall), axis=0)
        return jnp.where(line == packed_rows[0:bins], one, zero)

    def count_region(r):
        at = (r // 4 % 2 * (regions // 2) + r // 8 * 4 + r % 4) * coarse_bins
        count32[at : at + coarse_bins, :] = lax.dot_general(
            one_hot(coarse_spots, r, coarse_bins),
            one_hot(fine_spots, r, fine_bins),
            (((1,), (1,)), ((), ())),
            preferred_element_type=jnp.float32,
        )

    chunks = WIDTH // step
    for chunk in range(chunks):
        if chunk:
            trace_rows(chunk)
        for r in range(chunk * regions // chunks, (chunk + 1) * regions // chunks):
            count_region(r)
    for j in range(blocks):
        both = [count32[pl.ds(2 * j + q, regions, stride=coarse_bins), :] for q in range(2)]
        count16[j * LANES : (j + 1) * LANES, :] = jnp.transpose(
            jnp.concatenate(both, axis=1)
        ).astype(jnp.bfloat16)

    element = row_iota((WIDTH, regions))
    row = element // PROBE
    column = element & (PROBE - 1)
    place = lane_iota((8, regions))
    place = place % (regions // 2) // 4 * 8 + place // (regions // 2) * 4 + place % 4
    bounds = jnp.concatenate([aperture_ref[...], jnp.zeros((4, regions), jnp.int32)], axis=0)
    bounds = jnp.take_along_axis(bounds, place, axis=1)
    row_lo, row_hi = bounds[0:1, :] - first_row, bounds[1:2, :] - first_row
    col_lo, col_hi = bounds[2:3, :], bounds[3:4, :]
    column_inside = (column >= col_lo) & (column < col_hi)
    for which, delta in enumerate(DELTAS):
        other = column + delta
        inside = column_inside & (other >= col_lo) & (other < col_hi)
        colmask[which] = inside.astype(jnp.float32).astype(jnp.bfloat16)
    row_inside = (row >= row_lo) & (row < row_hi)
    for da in range(SUB):
        other = (row + da) & (SUB - 1)
        inside = row_inside & (other >= row_lo) & (other < row_hi)
        rowmask[da] = inside.astype(jnp.float32).astype(jnp.bfloat16)


    def gram_terms(which):
        delta = DELTAS[which]
        reach = SUB if delta else SUB // 2 + 1
        if which:
            for chunk in range(chunks):
                shift_rows(which, chunk)
        group = 4
        for begin in range(0, reach, group):
            held = range(begin, min(begin + group, reach))
            pairs = []
            for da in held:
                cut = WIDTH - da * PROBE
                pairs.append(shifted[0, 0:cut, :] * shifted[which, WIDTH - cut : WIDTH, :])
                if da:
                    pairs.append(shifted[0, cut:WIDTH, :] * shifted[which, 0 : WIDTH - cut, :])
            gram = jnp.dot(
                jnp.concatenate(pairs, axis=0), count16[...], preferred_element_type=jnp.float32
            ).astype(jnp.bfloat16)
            for n, da in enumerate(held):
                grams[which, da] = gram[n * WIDTH : (n + 1) * WIDTH] * colmask[which] * rowmask[da]

    def put(tile, terms):
        left = jnp.concatenate([windows[WINDOWS.index((delta, half, turn))] for delta, half, turn, da in terms], axis=1)
        right = jnp.concatenate([grams[DELTAS.index(delta), da] for delta, half, turn, da in terms], axis=0)
        out = jnp.dot(left, right, preferred_element_type=jnp.float32)
        out = jnp.transpose(out).astype(jnp.bfloat16)
        top, bottom = out[: regions // 2], out[regions // 2 :]
        at = (tile // (TILES // 2), slice(None), pl.ds(tile % (TILES // 2) * LANES, LANES))
        keep_ref[at] = jnp.where(core == 0, top, bottom)
        send_ref[at] = jnp.where(core == 0, bottom, top)

    for n, delta in enumerate((1, -7, 2, -6)):
        gram_terms(DELTAS.index(delta))
        for slot in range(4 * n, min(4 * n + 4, len(WINDOWS))):
            windows[slot] = window_matrix(*WINDOWS[slot])
    gram_terms(DELTAS.index(3))
    for da in range(SUB):
        put(da, ((1, 0, 0, da), (-7, 0, 0, da), (2, 1, 0, da), (-6, 1, 0, da)))
    gram_terms(DELTAS.index(-5))
    gram_terms(DELTAS.index(4))
    for da in range(SUB // 2):
        put(SUB + da, ((3, 0, 0, da), (-5, 0, 0, da), (3, 1, 0, da + 4), (-5, 1, 0, da + 4)))
    gram_terms(DELTAS.index(0))
    for da in range(SUB // 2):
        put(12 + da, ((4, 0, 0, da), (4, 0, da + 4, da + 4), (0, 1, 0, da)))
    put(16, ((0, 0, 0, 4),))
    last = (TILES // 2 - 1) * LANES
    for ref in (keep_ref, send_ref):
        ref[1, :, last:] = jnp.zeros((regions // 2, LANES), ref.dtype)


def stats(elem, reg, rf, tx_delay, rx_delay, aperture):
    regions = rx_delay.shape[0]
    samples = rf.shape[-1]
    voxels = tx_delay.shape[-1]
    vmem = pl.BlockSpec(memory_space=pltpu.VMEM)
    smem = pl.BlockSpec(memory_space=pltpu.SMEM)
    share = jax.ShapeDtypeStruct((2, regions // 2, TILES // 2 * LANES), jnp.bfloat16)
    return pl.pallas_call(
        stats_kernel,
        in_specs=[smem, smem, vmem, pl.BlockSpec(memory_space=pltpu.HBM), vmem, vmem],
        out_specs=[vmem] * 4,
        out_shape=[
            share,
            share,
            jax.ShapeDtypeStruct((WIDTH, samples), jnp.bfloat16),
            jax.ShapeDtypeStruct((regions, voxels), jnp.int32),
        ],
        scratch_shapes=[
            pltpu.VMEM((1, regions, voxels), tx_delay.dtype),
            pltpu.SemaphoreType.DMA,
            pltpu.VMEM((WIDTH + 2 * SUB, samples), jnp.float32),
            pltpu.VMEM((len(DELTAS), WIDTH, samples), jnp.bfloat16),
            pltpu.VMEM((samples // 64 * regions, 64), jnp.float32),
            pltpu.VMEM((samples, regions), jnp.bfloat16),
            pltpu.VMEM((len(DELTAS), WIDTH, regions), jnp.bfloat16),
            pltpu.VMEM((SUB, WIDTH, regions), jnp.bfloat16),
            pltpu.VMEM((len(WINDOWS), LANES, WIDTH), jnp.bfloat16),
            pltpu.VMEM((len(DELTAS), SUB, WIDTH, regions), jnp.bfloat16),
        ],
        compiler_params=pltpu.CompilerParams(vmem_limit_bytes=44 * 1024 * 1024),
        name="stats",
    )(elem, reg, rf, tx_delay, rx_delay, aperture)


def solve_kernel(total_ref, weights_ref):
    total = total_ref[...]
    per = TILES // 2
    tiles = [total[t // per : t // per + 1, t % per * LANES : (t % per + 1) * LANES] for t in range(TILES)]
    tall = jnp.concatenate(tiles + [jnp.zeros((LANES - TILES, LANES), jnp.float32)], axis=0)
    turned = jnp.transpose(tall)
    table = jnp.concatenate([turned[0:ORDER, 0:ORDER], turned[ORDER:LANES, 0:ORDER]], axis=1)
    i = row_iota((ORDER, LANES))
    lane = lane_iota((ORDER, LANES))
    j = lane & (ORDER - 1)
    da = ((j // SUB) - (i // SUB)) & (SUB - 1)
    d = ((j & (SUB - 1)) - (i & (SUB - 1))) & (SUB - 1)
    low = (i & (SUB - 1)) < 4
    spot = jnp.where(
        d == 1, da,
        jnp.where(
            d == 2, da + ORDER,
            jnp.where(
                d == 3, SUB + (da & 3) + ORDER * (da // 4),
                jnp.where(d == 4, jnp.where(low, 12 + da, 16 - da), jnp.where(da == 4, 16, 12 + da + ORDER)),
            ),
        ),
    )
    stored = ((d >= 1) & (d <= 3)) | ((d == 0) & (da <= 4))
    stored |= (d == 4) & ((low & (da <= 3)) | (~low & (da >= 1) & (da <= 4)))
    half = jnp.take_along_axis(table, spot & (LANES - 1), axis=1)
    half = jnp.where(stored & (lane < ORDER), half, 0.0)
    square = jnp.concatenate([half, jnp.zeros((LANES - ORDER, LANES), jnp.float32)], axis=0)
    cov = jnp.where(stored, half, jnp.transpose(square)[0:ORDER, :])
    diagonal = lane == i
    trace = jnp.sum(jnp.sum(jnp.where(diagonal, cov, 0.0), axis=1, keepdims=True), axis=0, keepdims=True)
    cov = cov + jnp.where(diagonal, load_factor * trace / ORDER, 0.0)
    work = jnp.where(lane < ORDER, cov, 1.0)
    high = 8
    shape = (high, LANES)
    sublane = row_iota(shape)
    groups = [work[g : g + high, :] for g in range(0, ORDER, high)]
    def spread(part, k):
        return jnp.broadcast_to(part[:, k : k + 1], shape)

    for k in range(0, ORDER, 4):
        at, inner = k // high, k % high
        rows = [jnp.broadcast_to(groups[at][inner + n : inner + n + 1, :], shape) for n in range(4)]
        m = [[spread(rows[n], k + c) for c in range(4)] for n in range(4)]
        inverse = 1.0 / (m[0][0] * m[1][1] - m[0][1] * m[1][0])
        i00, i01 = m[1][1] * inverse, -m[0][1] * inverse
        i10, i11 = -m[1][0] * inverse, m[0][0] * inverse
        e02, e03 = i00 * m[0][2] + i01 * m[1][2], i00 * m[0][3] + i01 * m[1][3]
        e12, e13 = i10 * m[0][2] + i11 * m[1][2], i10 * m[0][3] + i11 * m[1][3]
        first = i00 * rows[0] + i01 * rows[1]
        second = i10 * rows[0] + i11 * rows[1]
        third = rows[2] - m[2][0] * first - m[2][1] * second
        fourth = rows[3] - m[3][0] * first - m[3][1] * second
        s22 = m[2][2] - m[2][0] * e02 - m[2][1] * e12
        s23 = m[2][3] - m[2][0] * e03 - m[2][1] * e13
        s32 = m[3][2] - m[3][0] * e02 - m[3][1] * e12
        s33 = m[3][3] - m[3][0] * e03 - m[3][1] * e13
        inverse = 1.0 / (s22 * s33 - s23 * s32)
        third, fourth = (third * s33 - fourth * s23) * inverse, (fourth * s22 - third * s32) * inverse
        first = first - e02 * third - e03 * fourth
        second = second - e12 * third - e13 * fourth
        solved_rows = (first, second, third, fourth)
        updated = []
        for g, part in enumerate(groups):
            change = sum(spread(part, k + c) * solved_rows[c] for c in range(4))
            new = part - change
            if g == at:
                for c in range(4):
                    new = jnp.where(sublane == inner + c, solved_rows[c], new)
            updated.append(new)
        groups = updated
    solved = jnp.concatenate(groups, axis=0)[:, ORDER : ORDER + 1]
    row = jnp.sum(jnp.where(diagonal, solved, 0.0), axis=0, keepdims=True)
    weights_ref[...] = row / jnp.sum(row, axis=1, keepdims=True)


def solve(parts):
    return pl.pallas_call(
        solve_kernel,
        out_shape=jax.ShapeDtypeStruct((1, LANES), jnp.float32),
        compiler_params=pltpu.CompilerParams(vmem_limit_bytes=32 * 1024 * 1024),
        name="solve",
    )(parts)


def image_kernel(scale, elem, weights_ref, traces_ref, spots_ref, aperture_ref, out_ref, line_ref):
    regions, voxels = spots_ref.shape
    samples = traces_ref.shape[-1]
    first_row = elem[0] * SUB

    source = row_iota((LANES, WIDTH))
    element = lane_iota((LANES, WIDTH))
    x = source & (SUB - 1)
    k = element & (PROBE - 1)
    spread = (source // SUB == element // PROBE) & (k >= x) & (k <= x + PROBE - SUB)
    spread = spread.astype(jnp.float32).astype(jnp.bfloat16)
    weights = weights_ref[...]
    high, low = split(weights)
    gain = jnp.dot(high, spread, preferred_element_type=jnp.float32)
    gain = gain + jnp.dot(low, spread, preferred_element_type=jnp.float32)
    lane = lane_iota((regions, WIDTH))
    row = lane // PROBE + first_row
    column = lane & (PROBE - 1)
    bounds = aperture_ref[...].astype(jnp.float32)
    bounds = jnp.concatenate([bounds, jnp.zeros((LANES - 4, regions), jnp.float32)], axis=0)
    bounds = jnp.transpose(bounds).astype(jnp.int32)
    inside = (row >= bounds[:, 0:1]) & (row < bounds[:, 1:2])
    inside &= (column >= bounds[:, 2:3]) & (column < bounds[:, 3:4])
    high, low = split(jnp.where(inside, gain * scale, 0.0))
    both = jnp.dot(
        jnp.concatenate([high, low], axis=0), traces_ref[...], preferred_element_type=jnp.float32
    )
    line_ref[...] = both[:regions] + both[regions:]

    sums = spots_ref[...]
    own = out_ref.shape[2]
    group = 32
    blocks = samples // LANES
    near = 9
    for begin in range(0, regions, group):
        rows = slice(begin, begin + group)
        spots = sums[rows, :]
        first = jnp.minimum(jnp.min(spots, axis=1, keepdims=True) // LANES, blocks - near)
        first = jnp.broadcast_to(first, (group, LANES))
        parts = [line_ref[rows, j * LANES : (j + 1) * LANES] for j in range(blocks)]
        for bit in (4, 2, 1):
            here = (first & bit) != 0
            parts = [jnp.where(here, parts[j + bit], parts[j]) for j in range(near - 1 + bit)]
        for v in range(voxels // LANES):
            spot = spots[:, v * LANES : (v + 1) * LANES]
            fine = spot & (LANES - 1)
            coarse = spot // LANES - first
            picked = jnp.zeros((group, LANES), jnp.float32)
            for j in range(near):
                found = jnp.take_along_axis(parts[j], fine, axis=1)
                picked = jnp.where(coarse == j, found, picked)
            out_ref[begin // own : (begin + group) // own, v] = picked.reshape(group // own, own, LANES)


def image(scale, n_reg, elem, weights, traces, spots, aperture):
    regions, voxels = spots.shape
    samples = traces.shape[-1]
    vmem = pl.BlockSpec(memory_space=pltpu.VMEM)
    return pl.pallas_call(
        functools.partial(image_kernel, scale),
        in_specs=[pl.BlockSpec(memory_space=pltpu.SMEM), vmem, vmem, vmem, vmem],
        out_specs=vmem,
        out_shape=jax.ShapeDtypeStruct((n_reg, voxels // LANES, regions // n_reg, LANES), jnp.float32),
        scratch_shapes=[pltpu.VMEM((regions, samples), jnp.float32)],
        compiler_params=pltpu.CompilerParams(vmem_limit_bytes=32 * 1024 * 1024),
        name="image",
    )(elem, weights, traces, spots, aperture)


REG = ("xy", "core")
BOTH = ("xy", "core", "elem")
CHIPS = ("xy", "elem")


def per_device(rf, tx_delay, rx_delay, aperture):
    n_reg = lax.axis_size("xy") * lax.axis_size("core")
    n_elem = lax.axis_size("elem")
    regions, voxels = rx_delay.shape[0], tx_delay.shape[2]
    devices = n_reg * n_elem
    scale = 8.0 / math.sqrt(n_reg * n_elem * SHIFTS)
    elem = lax.axis_index("elem").astype(jnp.int32).reshape(1)
    reg = lax.axis_index(REG).astype(jnp.int32).reshape(1)
    bounds = aperture.T
    keep, send, traces, spots = stats(elem, reg, rf, tx_delay, rx_delay, bounds)
    other = lax.ppermute(send, "core", [(0, 1), (1, 0)])
    chip = (keep.astype(jnp.float32) + other.astype(jnp.float32)).astype(jnp.bfloat16)
    parts = lax.all_to_all(chip.transpose(1, 0, 2), CHIPS, 0, 0, tiled=True)
    mine = solve(jnp.sum(parts.astype(jnp.float32), axis=0))
    weights = lax.all_to_all(jnp.broadcast_to(mine, (devices, LANES)), BOTH, 0, 0, tiled=True)
    partial = image(scale, n_reg, elem, weights, traces, spots, bounds)
    owned = partial.reshape(devices, regions // n_reg, voxels // n_elem)
    arrived = lax.all_to_all(owned, BOTH, 0, 0, tiled=True)
    return jnp.sum(arrived, axis=0)


def solution(mesh):
    n_elem, n_reg = mesh.shape["elem"], mesh.shape["reg"]
    chips = jax.sharding.Mesh(mesh.devices.reshape(n_elem, n_reg // 2, 2), ("elem", "xy", "core"))
    in_specs = (P(REG, "elem", None), P(), P(None, "elem"), P())
    out_specs = P(REG, "elem")
    return jax.shard_map(
        per_device, mesh=chips, in_specs=in_specs, out_specs=out_specs, check_vma=False
    )
```
